128 devices in a mesh: block: 4 (over x), span: 8 (over z, core), stream: 4 (over y).
Axes of the slice: x: 4, y: 4, z: 4, core: 2. Of those that a mesh axis runs over, the one named last changes fastest.
Arguments:
- flow_state: float32 [4, 256, 16, 5, 4096], P('block', 'stream', None, None, 'span'), may hold values from -6 to 6
- wave_speed: float32 [4, 256, 16, 4096], P('block', 'stream', None, 'span'), may hold values from 0.5 to 2
- char_scale: float32 [5], replicated, may hold values from 0.002 to 4
- span_ratio: float32 [5], replicated, may hold values from 0.3 to 1
- send_tile: int32 [4, 8, 4, 32, 16], P('block', 'span', 'stream'), may hold values from 0 to 1023
- recv_tile: int32 [4, 8, 4, 32, 16], P('block', 'span', 'stream'), may hold values from 0 to 1023, as said below
- recv_live: int32 [4, 8, 4, 32, 16], P('block', 'span', 'stream'), may hold values from 0 to 1, as said below
- interp_weight: float32 [4, 8, 4, 32, 16], P('block', 'span', 'stream'), may hold values from 0.2 to 1
Outputs:
- new_state: float32 [4, 256, 16, 5, 4096], P('block', 'stream', None, None, 'span')
The draws below stay inside these ranges and needn't reach their ends.
Inputs may be any that keep to these rules, and one draw needn't show every extreme that they name: `recv_tile`: the 512 entries of one device are all different. `recv_live`: on each device the live slots from one peer come first; every device has 16 live slots from at least one peer, and one device has 16 from every peer.
All inputs are finite; a program needn't handle non-finite values.
Results may differ from the reference program's by a relative error of at most 0.000088.
Values sent between devices are 32-bit elements; how exact they have to be, the bound alone decides.
A program may use at most 256 MiB of HBM per device.

```python
import math
import jax
import jax.numpy as jnp
from jax import lax

VARS = 5
CAP = 16
CX = 64
CY = 16
CZ = 512
BLOCKS = 4
SLABS = 8
SECTIONS = 4
PEERS = 32
NX = 256
NZ = 4096


def draw_recv_tile(key, part):
    device_keys = jax.random.split(key, BLOCKS * SLABS * SECTIONS)

    def one_device(device_key):
        return jax.random.permutation(device_key, CX * CY)[:PEERS * CAP].astype(jnp.int32)
    picked = jax.vmap(one_device)(device_keys)
    return picked.reshape(BLOCKS, SLABS, SECTIONS, PEERS, CAP)


def draw_recv_live(key, part):
    key_count, key_heavy, key_full, key_device = jax.random.split(key, 4)
    counts = jax.random.randint(key_count, (BLOCKS, SLABS, SECTIONS, PEERS), 0, CAP + 1)
    heavy_block = jax.random.randint(key_heavy, (), 0, BLOCKS)
    block_index = jnp.arange(BLOCKS, dtype=jnp.int32)[:, None, None, None]
    counts = jnp.minimum(counts + jnp.where(block_index == heavy_block, CAP // 2, 0), CAP)
    full_peer = jax.random.randint(key_full, (BLOCKS, SLABS, SECTIONS, 1), 0, PEERS)
    peer_index = jnp.arange(PEERS, dtype=jnp.int32)
    counts = jnp.where(peer_index == full_peer, CAP, counts)
    full_device = jax.random.randint(key_device, (), 0, BLOCKS * SLABS * SECTIONS)
    device_index = jnp.arange(BLOCKS * SLABS * SECTIONS, dtype=jnp.int32).reshape(BLOCKS, SLABS, SECTIONS, 1)
    counts = jnp.where(device_index == full_device, CAP, counts)
    slot_index = jnp.arange(CAP, dtype=jnp.int32)
    return (slot_index < counts[..., None]).astype(jnp.int32)


def touch_ends(drawn, stream_key, least, high):
    longest = drawn.shape.index(max(drawn.shape))
    spots = []
    for shift in (0, 1):
        where = [jax.random.randint(jax.random.fold_in(stream_key, axis), (), 0, length) for axis, length in enumerate(drawn.shape)]
        where[longest] = (where[longest] + shift) % drawn.shape[longest]
        spots.append(tuple(where))
    return drawn.at[spots[0]].set(least).at[spots[1]].set(high)


def block_levels(stream_key, dims, shards, smallest, high):
    gain = 1.0
    for dim, blocks in shards:
        steps = jax.random.uniform(jax.random.fold_in(jax.random.fold_in(stream_key, 6), dim), (blocks,), jnp.float32, smallest / len(shards), high / len(shards))
        gain = gain * jnp.repeat(jnp.exp(steps), dims[dim] // blocks).reshape((-1,) + (1,) * (len(dims) - 1 - dim))
    return gain


def normal_values(own_key, dims, deviation, reach, cuts=(), held_as=jnp.bfloat16):
    array = jax.random.normal(own_key, dims, jnp.float32) * deviation
    if len(cuts) > 0:
        array = block_levels(own_key, dims, cuts, -0.22, 0.18) * array
    return jnp.clip(array, min=-reach, max=reach).astype(held_as)


def setup_inputs(seed: int = 0) -> dict:
    seeds = jax.random.split(jax.random.key(seed), 9)
    return {
        "flow_state": normal_values(seeds[0], (BLOCKS, NX, CY, VARS, NZ), 1.0, 6.0, ((0, 4), (1, 4), (4, 8)), jnp.float32),
        "wave_speed": jnp.clip(jnp.exp(math.log(2.0) - 1.3862944 * jax.random.uniform(seeds[1], (BLOCKS, NX, CY, NZ), jnp.float32) ** block_levels(seeds[1], (BLOCKS, NX, CY, NZ), ((0, 4), (1, 4), (3, 8)), -0.2, 0.2)), 0.5, 2.0),
        "char_scale": jnp.clip(jnp.exp(jax.random.uniform(seeds[2], (VARS,), jnp.float32, math.log(0.002), math.log(4.0))), 0.002, 4.0),
        "span_ratio": jnp.clip(jnp.exp(jax.random.uniform(seeds[3], (VARS,), jnp.float32, math.log(0.3), math.log(1.0))), 0.3, 1.0),
        "send_tile": touch_ends(jax.random.randint(seeds[4], (BLOCKS, SLABS, SECTIONS, PEERS, CAP), 0, CX * CY), jax.random.fold_in(seeds[4], 1), 0, (CX * CY) - 1).astype(jnp.int32),
        "recv_tile": draw_recv_tile(jax.random.fold_in(seeds[8], 71), 0),
        "recv_live": draw_recv_live(jax.random.fold_in(seeds[8], 71), 0),
        "interp_weight": jnp.clip(0.2 + 0.8 * jax.random.uniform(seeds[7], (BLOCKS, SLABS, SECTIONS, PEERS, CAP), jnp.float32) ** block_levels(seeds[7], (BLOCKS, SLABS, SECTIONS, PEERS, CAP), ((0, 4), (1, 8), (2, 4)), -0.2, 0.2), 0.2, 1.0),
    }


def minmod(first_diff, second_diff):
    return jnp.maximum(jnp.minimum(first_diff, second_diff), 0.0) + jnp.minimum(jnp.maximum(first_diff, second_diff), 0.0)


def face_value(behind, centre, forward):
    return centre + 0.5 * minmod(centre - behind, forward - centre)


def residual_of(padded, here_speed, prior_speed, rate_x, rate_z, width_x, width_z):
    def along_x(offset):
        return padded[:, 2 + offset:2 + offset + width_x, :, :, 2:2 + width_z]

    def along_z(offset):
        return padded[:, 2:2 + width_x, :, :, 2 + offset:2 + offset + width_z]

    right_x = rate_x * here_speed * face_value(along_x(-1), along_x(0), along_x(1))
    left_x = rate_x * prior_speed * face_value(along_x(-2), along_x(-1), along_x(0))
    right_z = rate_z * face_value(along_z(-1), along_z(0), along_z(1))
    left_z = rate_z * face_value(along_z(-2), along_z(-1), along_z(0))
    return left_x - right_x + left_z - right_z


def to_tiles(field):
    shaped = field.reshape(BLOCKS, SECTIONS, CX, CY, VARS, SLABS, CZ)
    shaped = jnp.transpose(shaped, (0, 5, 1, 2, 3, 4, 6))
    return shaped.reshape(BLOCKS * SLABS, SECTIONS, CX * CY, VARS, CZ)


def from_tiles(tile_rows):
    shaped = tile_rows.reshape(BLOCKS, SLABS, SECTIONS, CX, CY, VARS, CZ)
    shaped = jnp.transpose(shaped, (0, 2, 3, 4, 5, 1, 6))
    return shaped.reshape(BLOCKS, SECTIONS * CX, CY, VARS, SLABS * CZ)


def fill_fringe(flow_state, send_tile, recv_tile, recv_live, interp_weight):
    tile_rows = to_tiles(flow_state)
    sender_view = jnp.transpose(send_tile.reshape(PEERS, SECTIONS, PEERS, CAP), (2, 1, 0, 3))
    section_index = jnp.arange(SECTIONS, dtype=jnp.int32)[None, :, None, None]
    peer_index = jnp.arange(PEERS, dtype=jnp.int32)[None, None, :, None]
    owner_index = jnp.arange(PEERS, dtype=jnp.int32)[:, None, None, None]
    donors = tile_rows[peer_index, section_index, sender_view]
    targets = recv_tile.reshape(PEERS, SECTIONS, PEERS, CAP)
    previous = tile_rows[owner_index, section_index, targets]
    weight = interp_weight.reshape(PEERS, SECTIONS, PEERS, CAP)[..., None, None]
    live_mask = recv_live.reshape(PEERS, SECTIONS, PEERS, CAP)[..., None, None]
    blended = jnp.where(live_mask == 1, (1.0 - weight) * previous + weight * donors, previous)
    tile_rows = tile_rows.at[owner_index, section_index, targets].set(blended)
    return from_tiles(tile_rows)


def reference(flow_state, wave_speed, char_scale, span_ratio, send_tile, recv_tile, recv_live, interp_weight):
    filled = fill_fringe(flow_state, send_tile, recv_tile, recv_live, interp_weight)
    padded = jnp.pad(filled, ((0, 0), (2, 2), (0, 0), (0, 0), (2, 2)))
    speed_pad = jnp.pad(wave_speed, ((0, 0), (1, 0), (0, 0), (0, 0)))
    here_speed = wave_speed[:, :, :, None, :]
    prior_speed = speed_pad[:, :-1, :, None, :]
    rate_x = char_scale[:, None]
    rate_z = (char_scale * span_ratio)[:, None]
    residual = residual_of(padded, here_speed, prior_speed, rate_x, rate_z, NX, NZ)
    courant = 100.0 * rate_x * here_speed
    courant_prior = 100.0 * rate_x * prior_speed
    coupling = courant_prior / (1.0 + courant)
    source = 100.0 * residual / (1.0 + courant)

    def advance(running, inputs):
        running = inputs[0] * running + inputs[1]
        return running, running

    start = jnp.zeros((BLOCKS, CY, VARS, NZ), jnp.float32)
    _, marched = lax.scan(advance, start, (jnp.moveaxis(coupling, 1, 0), jnp.moveaxis(source, 1, 0)))
    return filled + jnp.moveaxis(marched, 0, 1)
```

```python
import functools

import jax
import jax.numpy as jnp
from jax import lax
from jax.experimental import pallas as pl
from jax.experimental.pallas import tpu as pltpu
from jax.sharding import PartitionSpec as P

MESH = pl.DeviceIdType.MESH
STRIDE = 11
UNROLL = 4


def limited(first_diff, second_diff):
    low = jnp.minimum(second_diff, 0.0)
    high = jnp.maximum(second_diff, 0.0)
    return jnp.minimum(jnp.maximum(first_diff, low), high)


def kernel(
    sizes,
    flow,
    speed,
    scale,
    ratio,
    send_tile,
    recv_tile,
    recv_live,
    weight,
    out,
    field,
    filled,
    donors,
    tiles,
    ws,
    inverse,
    growth,
    blend,
    sending,
    arriving,
    packed,
    row_low,
    row_high,
    col_low,
    col_high,
    last_update,
    last_growth,
    update_in,
    growth_in,
    slot_vmem,
    slot_of,
    load_sem,
    send_sem,
    recv_sem,
    halo_send,
    halo_recv,
    relay_send,
    relay_recv,
    out_sem,
    misc_sem,
):
    blocks, spans, streams = sizes
    width, parts, rows, lanes = flow.shape[0], flow.shape[1], flow.shape[2], 128
    peers = blocks * spans
    capacity = send_tile.shape[0]
    tiles_z = rows // 16
    chips = spans // 2
    message = capacity * tiles_z
    b = lax.axis_index("block")
    s = lax.axis_index("span")
    t = lax.axis_index("stream")
    me = b * spans + s
    z, core = s // 2, s % 2
    sign = 1 - 2 * core

    def partner(k):
        offset = (k * STRIDE) % peers
        to_block = (b + sign * (offset // spans) + blocks) % blocks
        to_chip = (z + sign * ((offset % spans) // 2) + chips) % chips
        to_core = (core + offset % 2) % 2
        return to_block, to_chip * 2 + to_core

    def at_stream(target):
        return (b, s, target)

    def load(v):
        return pltpu.make_async_copy(flow.at[:, v], field.at[v], load_sem.at[v])

    first_load = pltpu.make_async_copy(flow.at[:, 0], filled.at[pl.ds(0, width)], misc_sem.at[0])
    first_load.start()
    speed_load = pltpu.make_async_copy(speed, ws.at[pl.ds(1, width)], misc_sem.at[1])
    speed_load.start()
    for v in range(parts):
        load(v).start()

    barrier = pltpu.get_barrier_semaphore()

    def greet(k, carry):
        to_block, to_span = partner(k)
        pl.semaphore_signal(
            barrier, inc=1, device_id=(to_block, to_span, t), device_id_type=MESH
        )
        return carry

    lax.fori_loop(1, peers, greet, 0)
    for j in range(1, streams):
        pl.semaphore_signal(
            barrier, inc=1, device_id=at_stream((t + j) % streams), device_id_type=MESH
        )

    def donor_copy(v, k):
        to_block, to_span = partner(k)
        return pltpu.make_async_remote_copy(
            src_ref=sending.at[v, k],
            dst_ref=arriving.at[v, me],
            send_sem=send_sem.at[v],
            recv_sem=recv_sem.at[v],
            device_id=(to_block, to_span, t),
            device_id_type=MESH,
        )

    def send_all(v, source):
        def lay(x, carry):
            for y in range(16):
                row = pl.ds((y // 8) * 8 * tiles_z + y % 8, tiles_z, stride=8)
                tiles[x * 16 + y] = filled[x, row, :] if source is filled else source[v, x, row, :]
            return carry

        lax.fori_loop(0, width, lay, 0)
        for c in range(capacity):
            arriving[v, me, pl.ds(c * tiles_z, tiles_z), :] = tiles[send_tile[c, me]]

        def one(k, carry):
            to_block, to_span = partner(k)
            peer = to_block * spans + to_span
            for c in range(capacity):
                sending[v, k, pl.ds(c * tiles_z, tiles_z), :] = tiles[send_tile[c, peer]]
            donor_copy(v, k).start()
            return carry

        lax.fori_loop(1, peers, one, 0)

    first_load.wait()
    pl.semaphore_wait(barrier, peers - 1 + streams - 1)
    send_all(0, filled)

    speed_load.wait()
    speed_halo = pltpu.make_async_remote_copy(
        src_ref=ws.at[width],
        dst_ref=ws.at[0],
        send_sem=misc_sem.at[2],
        recv_sem=misc_sem.at[3],
        device_id=at_stream((t + 1) % streams),
        device_id_type=MESH,
    )

    @pl.when(t < streams - 1)
    def _():
        speed_halo.start()

    for v in range(parts):
        load(v).wait()
    send_all(1, field)

    @pl.when(t == 0)
    def _():
        ws[0] = jnp.zeros((rows, lanes), jnp.float32)
        row_low[...] = jnp.zeros(row_low.shape, jnp.float32)

    @pl.when(t == streams - 1)
    def _():
        row_high[...] = jnp.zeros(row_high.shape, jnp.float32)

    @pl.when(s == 0)
    def _():
        col_low[...] = jnp.zeros(col_low.shape, jnp.float32)

    @pl.when(s == spans - 1)
    def _():
        col_high[...] = jnp.zeros(col_high.shape, jnp.float32)

    lane = lax.broadcasted_iota(jnp.int32, (8, lanes), 1)
    tile_id = lane * 8 + lax.broadcasted_iota(jnp.int32, (8, lanes), 0)

    def place(g, carry):
        slots, weights = carry
        for c in range(capacity):
            target = jnp.where(recv_live[c, g] == 1, recv_tile[c, g], -1)
            hit = tile_id == target
            slots = jnp.where(hit, g * capacity + c, slots)
            weights = jnp.where(hit, weight[c, g], weights)
        return slots, weights

    slots, weights = lax.fori_loop(
        0,
        peers,
        place,
        (jnp.zeros((8, lanes), jnp.int32), jnp.zeros((8, lanes), jnp.float32)),
    )
    slot_vmem[...] = slots
    to_scalar = pltpu.make_async_copy(slot_vmem, slot_of, misc_sem.at[4])
    to_scalar.start()

    def spread(x, weights):
        for half in range(2):
            blend[x, pl.ds(half * 8, 8), :] = jnp.broadcast_to(weights[:, 0:1], (8, lanes))
            weights = pltpu.roll(weights, lanes - 1, 1)
        return weights

    lax.fori_loop(0, width, spread, weights)
    to_scalar.wait()

    @pl.when(t > 0)
    def _():
        speed_halo.wait_recv()

    tile_rows = [pl.ds(i * 8, 8) for i in range(rows // 8)]

    def factors(v):
        rate = scale[v]
        slot = v % 2

        def one(x, carry):
            new = []
            for i, r in enumerate(tile_rows):
                prior = rate * ws[x, r, :]
                here = rate * ws[x + 1, r, :]
                inv = 100.0 / (1.0 + 100.0 * here)
                inverse[x, r, :] = inv
                grown = carry[i] * (prior * inv)
                growth[slot, x, r, :] = grown
                new.append(grown)
            return tuple(new)

        ones = tuple(jnp.ones((8, lanes), jnp.float32) for _ in tile_rows)
        ended = lax.fori_loop(0, width, one, ones)
        for r, grown in zip(tile_rows, ended):
            last_growth[v, r, :] = grown

    def relay(v, kind, j):
        source = last_growth if kind else last_update
        target = growth_in if kind else update_in
        return pltpu.make_async_remote_copy(
            src_ref=source.at[v],
            dst_ref=target.at[v, t],
            send_sem=relay_send.at[v, kind, j],
            recv_sem=relay_recv.at[v, kind, t],
            device_id=at_stream((t + j) % streams),
            device_id_type=MESH,
        )

    def relay_from(v, kind, source):
        target = growth_in if kind else update_in
        return pltpu.make_async_copy(
            target.at[v, source], target.at[v, source], relay_recv.at[v, kind, source]
        )

    def relay_all(v, kind):
        for j in range(1, streams):

            @pl.when(t + j < streams)
            def _():
                relay(v, kind, j).start()

    def fill(v):
        def take_peer(g, carry):
            for c in range(capacity):
                donors[g * capacity + c] = arriving[v, g, pl.ds(c * tiles_z, tiles_z), :]
            return carry

        lax.fori_loop(0, peers, take_peer, 0)

        def scatter(x, carry):
            for y in range(16):
                row = pl.ds((y // 8) * 8 * tiles_z + y % 8, tiles_z, stride=8)
                filled[x, row, :] = donors[slot_of[y % 8, x * 2 + y // 8]]
            return carry

        lax.fori_loop(0, width, scatter, 0)

        def mix(x, carry):
            first, before, last = carry
            for half in range(2):
                w = blend[x, pl.ds(half * 8, 8), :]
                rest = 1.0 - w
                kept = []
                for i in range(tiles_z):
                    r = tile_rows[half * tiles_z + i]
                    value = rest * field[v, x, r, :] + w * filled[x, r, :]
                    filled[x, r, :] = value
                    kept.append(value)
                i = x * 2 + half
                here = lane == i
                first = jnp.where(here, pltpu.roll(kept[0], i, 1), first)
                before = jnp.where(here, pltpu.roll(kept[-1], (i + 2) % lanes, 1), before)
                last = jnp.where(here, pltpu.roll(kept[-1], (i + 1) % lanes, 1), last)
            return first, before, last

        zero = jnp.zeros((8, lanes), jnp.float32)
        for i, value in enumerate(lax.fori_loop(0, width, mix, (zero, zero, zero))):
            packed[v, i] = value

    def halo_copy(v, kind):
        src, dst, target = (
            (filled.at[pl.ds(width - 2, 2)], row_low.at[v], (b, s, (t + 1) % streams)),
            (filled.at[0], row_high.at[v], (b, s, (t + streams - 1) % streams)),
            (packed.at[v, pl.ds(1, 2)], col_low.at[v], (b, (s + 1) % spans, t)),
            (packed.at[v, 0], col_high.at[v], (b, (s + spans - 1) % spans, t)),
        )[kind]
        return pltpu.make_async_remote_copy(
            src_ref=src,
            dst_ref=dst,
            send_sem=halo_send.at[v, kind],
            recv_sem=halo_recv.at[v, kind],
            device_id=target,
            device_id_type=MESH,
        )

    sends = (t < streams - 1, t > 0, s < spans - 1, s > 0)
    receives = (t > 0, t < streams - 1, s > 0, s < spans - 1)

    def halos(v, which, act):
        for kind in range(4):

            @pl.when(which[kind])
            def _():
                act(halo_copy(v, kind))

    def sweep(v):
        rate = scale[v]
        rate_z = rate * ratio[v]
        is_first = lane == 0
        is_last = lane == lanes - 1
        before2, before1, after1 = col_low[v, 0], col_low[v, 1], col_high[v]
        edge_first = packed[v, 0] - before1
        edge_face = before1 + 0.5 * limited(before1 - before2, edge_first)
        edge_last = after1 - packed[v, 2]
        for i, r in enumerate(tile_rows):
            filled[width, r, :] = row_high[v, r, :]

        for half in range(2):
            mine = tile_rows[half * tiles_z : (half + 1) * tiles_z]

            def step(x, carry, end):
                cells, diffs, flux, e_first, e_face, e_last = carry
                n = range(tiles_z)
                right = [pltpu.roll(u, 1, 1) for u in cells]
                e = [
                    cells[i] - jnp.where(is_first, right[i - 1], right[i]) if i else None for i in n
                ]
                e[0] = jnp.where(is_first, e_first, cells[0] - right[0])
                left = [pltpu.roll(d, lanes - 1, 1) for d in e]
                ahead = [
                    jnp.where(is_last, left[i + 1] if i + 1 < tiles_z else e_last, left[i])
                    for i in n
                ]
                face = [cells[i] + 0.5 * limited(e[i], ahead[i]) for i in n]
                shifted = [pltpu.roll(f, 1, 1) for f in face]
                behind = [
                    jnp.where(is_first, shifted[i - 1] if i else e_face, shifted[i]) for i in n
                ]
                span_term = [rate_z * (behind[i] - face[i]) for i in n]
                coming = [filled[x + 1, r, :] for r in mine]
                next_diffs = [coming[i] - cells[i] for i in n]
                face_x = [cells[i] + 0.5 * limited(diffs[i], next_diffs[i]) for i in n]
                speed_x = [rate * ws[x + 1, r, :] for r in mine]
                rest = [span_term[i] - speed_x[i] * face_x[i] for i in n]
                update = [inverse[x, r, :] * (flux[i] + rest[i]) for i, r in enumerate(mine)]
                next_flux = [speed_x[i] * (update[i] + face_x[i]) for i in n]
                for i, r in enumerate(mine):
                    field[v, x, r, :] = cells[i] + update[i]
                    if end:
                        last_update[v, r, :] = update[i]
                return (
                    coming,
                    next_diffs,
                    next_flux,
                    pltpu.roll(e_first, lanes - 2, 1),
                    pltpu.roll(e_face, lanes - 2, 1),
                    pltpu.roll(e_last, lanes - 2, 1),
                )

            def steps(outer, carry):
                for k in range(UNROLL):
                    carry = step(outer * UNROLL + k, carry, k == UNROLL - 1)
                return carry

            cells = [filled[0, r, :] for r in mine]
            up1 = [row_low[v, 1, r, :] for r in mine]
            up2 = [row_low[v, 0, r, :] for r in mine]
            diffs = [c - u for c, u in zip(cells, up1)]
            flux = [
                rate * ws[0, r, :] * (u + 0.5 * limited(u - u2, d))
                for r, u, u2, d in zip(mine, up1, up2, diffs)
            ]

            def turned(value, shift):
                return pltpu.roll(value, shift, 1) if shift else value

            lax.fori_loop(
                0,
                width // UNROLL,
                steps,
                (
                    cells,
                    diffs,
                    flux,
                    turned(edge_first, (lanes - half) % lanes),
                    turned(edge_face, (lanes - half) % lanes),
                    turned(edge_last, lanes - 1 - half),
                ),
            )

    def finish(v):
        slot = v % 2
        for j in range(streams - 1):

            @pl.when(j < t)
            def _():
                relay_from(v, 0, j).wait()
                relay_from(v, 1, j).wait()

        inflow = [jnp.zeros((8, lanes), jnp.float32) for _ in tile_rows]
        for j in range(streams - 1):
            inflow = [
                jnp.where(
                    j < t, growth_in[v, j, r, :] * inflow[i] + update_in[v, j, r, :], inflow[i]
                )
                for i, r in enumerate(tile_rows)
            ]

        def one(x, carry):
            for i, r in enumerate(tile_rows):
                field[v, x, r, :] = field[v, x, r, :] + growth[slot, x, r, :] * inflow[i]
            return carry

        lax.fori_loop(0, width, one, 0)
        out_copy(v).start()

    def out_copy(v):
        return pltpu.make_async_copy(field.at[v], out.at[:, v], out_sem.at[v])

    def all_donors(v):
        return pltpu.make_async_remote_copy(
            src_ref=sending.at[v, pl.ds(1, peers - 1)],
            dst_ref=arriving.at[v, pl.ds(0, peers - 1)],
            send_sem=send_sem.at[v],
            recv_sem=recv_sem.at[v],
            device_id=(b, s, (t + 1) % streams),
            device_id_type=MESH,
        )

    def variable(v, carry):
        factors(v)
        relay_all(v, 1)
        all_donors(v).wait_recv()
        fill(v)
        halos(v, sends, lambda copy: copy.start())

        @pl.when(v + 2 < parts)
        def _():
            send_all(v + 2, field)

        @pl.when(v > 0)
        def _():
            finish(v - 1)

        halos(v, receives, lambda copy: copy.wait_recv())
        sweep(v)
        relay_all(v, 0)
        halos(v, sends, lambda copy: copy.wait_send())
        return carry

    lax.fori_loop(0, parts, variable, 0)
    finish(parts - 1)

    for v in range(parts):
        all_donors(v).wait_send()
        for kind in range(2):
            for j in range(1, streams):

                @pl.when(t + j < streams)
                def _():
                    relay(v, kind, j).wait_send()

        out_copy(v).wait()

    @pl.when(t < streams - 1)
    def _():
        speed_halo.wait_send()


def on_device(
    flow_state, wave_speed, char_scale, span_ratio, send_tile, recv_tile, recv_live, interp_weight
):
    sizes = tuple(lax.axis_size(a) for a in ("block", "span", "stream"))
    blocks, spans, streams = sizes
    _, width, rows_y, parts, width_z = flow_state.shape
    tiles_z = width_z // 128
    rows = rows_y * tiles_z
    capacity = send_tile.shape[-1]
    peers = blocks * spans

    def tiled(array):
        lead = array.shape[:-2]
        array = array.reshape(lead + (rows_y // 8, 8, tiles_z, 128))
        return jnp.swapaxes(array, -3, -2).reshape(lead + (rows, 128))

    flow = tiled(jnp.transpose(flow_state[0], (0, 2, 1, 3)))
    speed = tiled(wave_speed[0])
    small = [
        jnp.transpose(a.reshape(peers, capacity))
        for a in (send_tile, recv_tile, recv_live, interp_weight)
    ]
    f32 = jnp.float32
    anywhere = pl.BlockSpec(memory_space=pl.ANY)
    scalars = pl.BlockSpec(memory_space=pltpu.SMEM)
    message = capacity * tiles_z
    vmem = lambda *shape: pltpu.VMEM(shape, f32)
    dma = pltpu.SemaphoreType.DMA
    result = pl.pallas_call(
        functools.partial(kernel, sizes),
        out_shape=jax.ShapeDtypeStruct(flow.shape, f32),
        in_specs=[anywhere, anywhere] + [scalars] * 6,
        out_specs=anywhere,
        scratch_shapes=[
            vmem(parts, width, rows, 128),
            vmem(width + 1, rows, 128),
            vmem(peers * capacity, tiles_z, 128),
            vmem(width * rows_y, tiles_z, 128),
            vmem(width + 1, rows, 128),
            vmem(width, rows, 128),
            vmem(2, width, rows, 128),
            vmem(width, rows_y, 128),
            vmem(parts, peers, message, 128),
            vmem(parts, peers, message, 128),
            vmem(parts, 3, 8, 128),
            vmem(parts, 2, rows, 128),
            vmem(parts, rows, 128),
            vmem(parts, 2, 8, 128),
            vmem(parts, 8, 128),
            vmem(parts, rows, 128),
            vmem(parts, rows, 128),
            vmem(parts, streams, rows, 128),
            vmem(parts, streams, rows, 128),
            pltpu.VMEM((8, 128), jnp.int32),
            pltpu.SMEM((8, 128), jnp.int32),
            dma((parts,)),
            dma((parts,)),
            dma((parts,)),
            dma((parts, 4)),
            dma((parts, 4)),
            dma((parts, 2, streams)),
            dma((parts, 2, streams)),
            dma((parts,)),
            dma((5,)),
        ],
        compiler_params=pltpu.CompilerParams(
            collective_id=1, has_side_effects=True, vmem_limit_bytes=56 * 1024 * 1024
        ),
        name="overset_step",
    )(flow, speed, char_scale, span_ratio, *small)
    result = result.reshape(width, parts, rows_y // 8, tiles_z, 8, 128)
    result = jnp.swapaxes(result, 3, 4).reshape(width, parts, rows_y, width_z)
    return jnp.transpose(result, (0, 2, 1, 3))[None]


def solution(mesh):
    return jax.shard_map(
        on_device,
        mesh=mesh,
        in_specs=(
            P("block", "stream", None, None, "span"),
            P("block", "stream", None, "span"),
            P(),
            P(),
            P("block", "span", "stream", None, None),
            P("block", "span", "stream", None, None),
            P("block", "span", "stream", None, None),
            P("block", "span", "stream", None, None),
        ),
        out_specs=P("block", "stream", None, None, "span"),
        check_vma=False,
    )
```

```python
import functools

import jax
import jax.numpy as jnp
from jax import lax
from jax.experimental import pallas as pl
from jax.experimental.pallas import tpu as pltpu
from jax.sharding import PartitionSpec as P

MESH = pl.DeviceIdType.MESH
STRIDE = 11
UNROLL = 8
TURN = 4


def limited(first_diff, second_diff):
    low = jnp.minimum(second_diff, 0.0)
    high = jnp.maximum(second_diff, 0.0)
    return jnp.minimum(jnp.maximum(first_diff, low), high)


def kernel(
    sizes,
    flow,
    speed,
    scale,
    ratio,
    send_tile,
    recv_tile,
    recv_live,
    weight,
    out,
    field,
    filled,
    donors,
    tiles,
    ws,
    inverse,
    growth,
    blend,
    sending,
    arriving,
    packed,
    row_low,
    row_high,
    col_low,
    col_high,
    last_update,
    last_growth,
    update_in,
    growth_in,
    slot_vmem,
    slot_of,
    load_sem,
    send_sem,
    recv_sem,
    halo_send,
    halo_recv,
    relay_send,
    relay_recv,
    out_sem,
    misc_sem,
):
    blocks, spans, streams = sizes
    width, parts, rows, lanes = flow.shape[0], flow.shape[1], flow.shape[2], 128
    peers = blocks * spans
    capacity = send_tile.shape[0]
    tiles_z = rows // 16
    chips = spans // 2
    message = capacity * tiles_z
    b = lax.axis_index("block")
    s = lax.axis_index("span")
    t = lax.axis_index("stream")
    me = b * spans + s
    z, core = s // 2, s % 2
    sign = 1 - 2 * core

    def partner(k):
        offset = (k * STRIDE) % peers
        to_block = (b + sign * (offset // spans) + blocks) % blocks
        to_chip = (z + sign * ((offset % spans) // 2) + chips) % chips
        to_core = (core + offset % 2) % 2
        return to_block, to_chip * 2 + to_core

    def at_stream(target):
        return (b, s, target)

    def load(v):
        return pltpu.make_async_copy(flow.at[:, v], field.at[v], load_sem.at[v])

    first_load = pltpu.make_async_copy(flow.at[:, 0], filled.at[pl.ds(0, width)], misc_sem.at[0])
    first_load.start()
    speed_load = pltpu.make_async_copy(speed, ws.at[pl.ds(1, width)], misc_sem.at[1])
    speed_load.start()
    for v in range(parts):
        load(v).start()

    barrier = pltpu.get_barrier_semaphore()

    def greet(k, carry):
        to_block, to_span = partner(k)
        pl.semaphore_signal(
            barrier, inc=1, device_id=(to_block, to_span, t), device_id_type=MESH
        )
        return carry

    lax.fori_loop(1, peers, greet, 0)
    for j in range(1, streams):
        pl.semaphore_signal(
            barrier, inc=1, device_id=at_stream((t + j) % streams), device_id_type=MESH
        )

    def donor_copy(v, k):
        to_block, to_span = partner(k)
        return pltpu.make_async_remote_copy(
            src_ref=sending.at[v, k],
            dst_ref=arriving.at[v, me],
            send_sem=send_sem.at[v],
            recv_sem=recv_sem.at[v],
            device_id=(to_block, to_span, t),
            device_id_type=MESH,
        )

    def send_all(v, source):
        def lay(x, carry):
            for y in range(16):
                row = pl.ds((y // 8) * 8 * tiles_z + y % 8, tiles_z, stride=8)
                tiles[x * 16 + y] = filled[x, row, :] if source is filled else source[v, x, row, :]
            return carry

        lax.fori_loop(0, width, lay, 0)
        for c in range(capacity):
            arriving[v, me, pl.ds(c * tiles_z, tiles_z), :] = tiles[send_tile[c, me]]

        def one(k, carry):
            to_block, to_span = partner(k)
            peer = to_block * spans + to_span
            for c in range(capacity):
                sending[v, k, pl.ds(c * tiles_z, tiles_z), :] = tiles[send_tile[c, peer]]
            donor_copy(v, k).start()
            return carry

        lax.fori_loop(1, peers, one, 0)

    first_load.wait()
    pl.semaphore_wait(barrier, peers - 1 + streams - 1)
    send_all(0, filled)

    speed_load.wait()
    speed_halo = pltpu.make_async_remote_copy(
        src_ref=ws.at[width],
        dst_ref=ws.at[0],
        send_sem=misc_sem.at[2],
        recv_sem=misc_sem.at[3],
        device_id=at_stream((t + 1) % streams),
        device_id_type=MESH,
    )

    @pl.when(t < streams - 1)
    def _():
        speed_halo.start()

    for v in range(parts):
        load(v).wait()
    send_all(1, field)

    @pl.when(t == 0)
    def _():
        ws[0] = jnp.zeros((rows, lanes), jnp.float32)
        row_low[...] = jnp.zeros(row_low.shape, jnp.float32)

    @pl.when(t == streams - 1)
    def _():
        row_high[...] = jnp.zeros(row_high.shape, jnp.float32)

    @pl.when(s == 0)
    def _():
        col_low[...] = jnp.zeros(col_low.shape, jnp.float32)

    @pl.when(s == spans - 1)
    def _():
        col_high[...] = jnp.zeros(col_high.shape, jnp.float32)

    lane = lax.broadcasted_iota(jnp.int32, (8, lanes), 1)
    tile_id = lane * 8 + lax.broadcasted_iota(jnp.int32, (8, lanes), 0)

    def place(g, carry):
        slots, weights = carry
        for c in range(capacity):
            target = jnp.where(recv_live[c, g] == 1, recv_tile[c, g], -1)
            hit = tile_id == target
            slots = jnp.where(hit, g * capacity + c, slots)
            weights = jnp.where(hit, weight[c, g], weights)
        return slots, weights

    slots, weights = lax.fori_loop(
        0,
        peers,
        place,
        (jnp.zeros((8, lanes), jnp.int32), jnp.zeros((8, lanes), jnp.float32)),
    )
    slot_vmem[...] = slots
    to_scalar = pltpu.make_async_copy(slot_vmem, slot_of, misc_sem.at[4])
    to_scalar.start()

    def spread(outer, weights):
        for k in range(2 * TURN):
            i = outer * 2 * TURN + k
            turned = pltpu.roll(weights, (lanes - i) % lanes, 1)
            blend[outer * TURN + k // 2, pl.ds(k % 2 * 8, 8), :] = jnp.broadcast_to(
                turned[:, 0:1], (8, lanes)
            )
        return weights

    lax.fori_loop(0, width // TURN, spread, weights)
    to_scalar.wait()

    @pl.when(t > 0)
    def _():
        speed_halo.wait_recv()

    tile_rows = [pl.ds(i * 8, 8) for i in range(rows // 8)]

    def factors(v):
        rate = scale[v]
        slot = v % 2

        def one(x, carry):
            new = []
            for i, r in enumerate(tile_rows):
                prior = rate * ws[x, r, :]
                here = rate * ws[x + 1, r, :]
                inv = 100.0 / (1.0 + 100.0 * here)
                inverse[x, r, :] = inv
                grown = carry[i] * (prior * inv)
                growth[slot, x, r, :] = grown
                new.append(grown)
            return tuple(new)

        ones = tuple(jnp.ones((8, lanes), jnp.float32) for _ in tile_rows)
        ended = lax.fori_loop(0, width, one, ones)
        for r, grown in zip(tile_rows, ended):
            last_growth[v, r, :] = grown

    def relay(v, kind, j):
        source = last_growth if kind else last_update
        target = growth_in if kind else update_in
        return pltpu.make_async_remote_copy(
            src_ref=source.at[v],
            dst_ref=target.at[v, t],
            send_sem=relay_send.at[v, kind, j],
            recv_sem=relay_recv.at[v, kind, t],
            device_id=at_stream((t + j) % streams),
            device_id_type=MESH,
        )

    def relay_from(v, kind, source):
        target = growth_in if kind else update_in
        return pltpu.make_async_copy(
            target.at[v, source], target.at[v, source], relay_recv.at[v, kind, source]
        )

    def relay_all(v, kind):
        for j in range(1, streams):

            @pl.when(t + j < streams)
            def _():
                relay(v, kind, j).start()

    def fill(v):
        def take_peer(g, carry):
            for c in range(capacity):
                donors[g * capacity + c] = arriving[v, g, pl.ds(c * tiles_z, tiles_z), :]
            return carry

        lax.fori_loop(0, peers, take_peer, 0)

        def scatter(x, carry):
            for y in range(16):
                row = pl.ds((y // 8) * 8 * tiles_z + y % 8, tiles_z, stride=8)
                filled[x, row, :] = donors[slot_of[y % 8, x * 2 + y // 8]]
            return carry

        lax.fori_loop(0, width, scatter, 0)

        def mix(outer, carry):
            first, before, last = carry
            for k in range(2 * TURN):
                x, half = outer * TURN + k // 2, k % 2
                w = blend[x, pl.ds(half * 8, 8), :]
                rest = 1.0 - w
                kept = []
                for i in range(tiles_z):
                    r = tile_rows[half * tiles_z + i]
                    value = rest * field[v, x, r, :] + w * filled[x, r, :]
                    filled[x, r, :] = value
                    kept.append(value)
                i = outer * 2 * TURN + k
                here = lane == i
                first = jnp.where(here, pltpu.roll(kept[0], i, 1), first)
                before = jnp.where(here, pltpu.roll(kept[-1], (i + 2) % lanes, 1), before)
                last = jnp.where(here, pltpu.roll(kept[-1], (i + 1) % lanes, 1), last)
            return first, before, last

        zero = jnp.zeros((8, lanes), jnp.float32)
        for i, value in enumerate(lax.fori_loop(0, width // TURN, mix, (zero, zero, zero))):
            packed[v, i] = value

    def halo_copy(v, kind):
        src, dst, target = (
            (filled.at[pl.ds(width - 2, 2)], row_low.at[v], (b, s, (t + 1) % streams)),
            (filled.at[0], row_high.at[v], (b, s, (t + streams - 1) % streams)),
            (packed.at[v, pl.ds(1, 2)], col_low.at[v], (b, (s + 1) % spans, t)),
            (packed.at[v, 0], col_high.at[v], (b, (s + spans - 1) % spans, t)),
        )[kind]
        return pltpu.make_async_remote_copy(
            src_ref=src,
            dst_ref=dst,
            send_sem=halo_send.at[v, kind],
            recv_sem=halo_recv.at[v, kind],
            device_id=target,
            device_id_type=MESH,
        )

    sends = (t < streams - 1, t > 0, s < spans - 1, s > 0)
    receives = (t > 0, t < streams - 1, s > 0, s < spans - 1)

    def halos(v, which, act):
        for kind in range(4):

            @pl.when(which[kind])
            def _():
                act(halo_copy(v, kind))

    def sweep(v):
        rate = scale[v]
        rate_z = rate * ratio[v]
        is_first = lane == 0
        is_last = lane == lanes - 1
        before2, before1, after1 = col_low[v, 0], col_low[v, 1], col_high[v]
        edge_face = before1 + 0.5 * limited(before1 - before2, packed[v, 0] - before1)
        for i, r in enumerate(tile_rows):
            filled[width, r, :] = row_high[v, r, :]

        for half in range(2):
            mine = tile_rows[half * tiles_z : (half + 1) * tiles_z]

            def step(x, carry, end):
                cells, diffs, flux = carry
                n = range(tiles_z)
                i = x * 2 + half
                to_first = (lanes - i) % lanes
                outside = pltpu.roll(before1, to_first, 1)
                outside_face = pltpu.roll(edge_face, to_first, 1)
                beyond = pltpu.roll(after1, lanes - 1 - i, 1)
                right = [pltpu.roll(u, 1, 1) for u in cells]
                left = [pltpu.roll(u, lanes - 1, 1) for u in cells]
                low = [jnp.where(is_first, ([outside] + right)[i], right[i]) for i in n]
                high = [jnp.where(is_last, (left + [beyond])[i + 1], left[i]) for i in n]
                face = [
                    cells[i] + 0.5 * limited(cells[i] - low[i], high[i] - cells[i]) for i in n
                ]
                shifted = [pltpu.roll(f, 1, 1) for f in face]
                behind = [
                    jnp.where(is_first, ([outside_face] + shifted)[i], shifted[i]) for i in n
                ]
                span_term = [rate_z * (behind[i] - face[i]) for i in n]
                coming = [filled[x + 1, r, :] for r in mine]
                next_diffs = [coming[i] - cells[i] for i in n]
                face_x = [cells[i] + 0.5 * limited(diffs[i], next_diffs[i]) for i in n]
                speed_x = [rate * ws[x + 1, r, :] for r in mine]
                rest = [span_term[i] - speed_x[i] * face_x[i] for i in n]
                update = [inverse[x, r, :] * (flux[i] + rest[i]) for i, r in enumerate(mine)]
                next_flux = [speed_x[i] * (update[i] + face_x[i]) for i in n]
                for i, r in enumerate(mine):
                    field[v, x, r, :] = cells[i] + update[i]
                    if end:
                        last_update[v, r, :] = update[i]
                return coming, next_diffs, next_flux

            def steps(outer, carry):
                for k in range(UNROLL):
                    carry = step(outer * UNROLL + k, carry, k == UNROLL - 1)
                return carry

            cells = [filled[0, r, :] for r in mine]
            up1 = [row_low[v, 1, r, :] for r in mine]
            up2 = [row_low[v, 0, r, :] for r in mine]
            diffs = [c - u for c, u in zip(cells, up1)]
            flux = [
                rate * ws[0, r, :] * (u + 0.5 * limited(u - u2, d))
                for r, u, u2, d in zip(mine, up1, up2, diffs)
            ]

            lax.fori_loop(0, width // UNROLL, steps, (cells, diffs, flux))

    def finish(v):
        slot = v % 2
        for j in range(streams - 1):

            @pl.when(j < t)
            def _():
                relay_from(v, 0, j).wait()
                relay_from(v, 1, j).wait()

        inflow = [jnp.zeros((8, lanes), jnp.float32) for _ in tile_rows]
        for j in range(streams - 1):
            inflow = [
                jnp.where(
                    j < t, growth_in[v, j, r, :] * inflow[i] + update_in[v, j, r, :], inflow[i]
                )
                for i, r in enumerate(tile_rows)
            ]

        def one(x, carry):
            for i, r in enumerate(tile_rows):
                field[v, x, r, :] = field[v, x, r, :] + growth[slot, x, r, :] * inflow[i]
            return carry

        lax.fori_loop(0, width, one, 0)
        out_copy(v).start()

    def out_copy(v):
        return pltpu.make_async_copy(field.at[v], out.at[:, v], out_sem.at[v])

    def all_donors(v):
        return pltpu.make_async_remote_copy(
            src_ref=sending.at[v, pl.ds(1, peers - 1)],
            dst_ref=arriving.at[v, pl.ds(0, peers - 1)],
            send_sem=send_sem.at[v],
            recv_sem=recv_sem.at[v],
            device_id=(b, s, (t + 1) % streams),
            device_id_type=MESH,
        )

    def variable(v, carry):
        factors(v)
        relay_all(v, 1)
        all_donors(v).wait_recv()
        fill(v)
        halos(v, sends, lambda copy: copy.start())

        @pl.when(v + 2 < parts)
        def _():
            send_all(v + 2, field)

        @pl.when(v > 0)
        def _():
            finish(v - 1)

        halos(v, receives, lambda copy: copy.wait_recv())
        sweep(v)
        relay_all(v, 0)
        halos(v, sends, lambda copy: copy.wait_send())
        return carry

    lax.fori_loop(0, parts, variable, 0)
    finish(parts - 1)

    for v in range(parts):
        all_donors(v).wait_send()
        for kind in range(2):
            for j in range(1, streams):

                @pl.when(t + j < streams)
                def _():
                    relay(v, kind, j).wait_send()

        out_copy(v).wait()

    @pl.when(t < streams - 1)
    def _():
        speed_halo.wait_send()


def on_device(
    flow_state, wave_speed, char_scale, span_ratio, send_tile, recv_tile, recv_live, interp_weight
):
    sizes = tuple(lax.axis_size(a) for a in ("block", "span", "stream"))
    blocks, spans, streams = sizes
    _, width, rows_y, parts, width_z = flow_state.shape
    tiles_z = width_z // 128
    rows = rows_y * tiles_z
    capacity = send_tile.shape[-1]
    peers = blocks * spans

    def tiled(array):
        lead = array.shape[:-2]
        array = array.reshape(lead + (rows_y // 8, 8, tiles_z, 128))
        return jnp.swapaxes(array, -3, -2).reshape(lead + (rows, 128))

    flow = tiled(jnp.transpose(flow_state[0], (0, 2, 1, 3)))
    speed = tiled(wave_speed[0])
    small = [
        jnp.transpose(a.reshape(peers, capacity))
        for a in (send_tile, recv_tile, recv_live, interp_weight)
    ]
    f32 = jnp.float32
    anywhere = pl.BlockSpec(memory_space=pl.ANY)
    scalars = pl.BlockSpec(memory_space=pltpu.SMEM)
    message = capacity * tiles_z
    vmem = lambda *shape: pltpu.VMEM(shape, f32)
    dma = pltpu.SemaphoreType.DMA
    result = pl.pallas_call(
        functools.partial(kernel, sizes),
        out_shape=jax.ShapeDtypeStruct(flow.shape, f32),
        in_specs=[anywhere, anywhere] + [scalars] * 6,
        out_specs=anywhere,
        scratch_shapes=[
            vmem(parts, width, rows, 128),
            vmem(width + 1, rows, 128),
            vmem(peers * capacity, tiles_z, 128),
            vmem(width * rows_y, tiles_z, 128),
            vmem(width + 1, rows, 128),
            vmem(width, rows, 128),
            vmem(2, width, rows, 128),
            vmem(width, rows_y, 128),
            vmem(parts, peers, message, 128),
            vmem(parts, peers, message, 128),
            vmem(parts, 3, 8, 128),
            vmem(parts, 2, rows, 128),
            vmem(parts, rows, 128),
            vmem(parts, 2, 8, 128),
            vmem(parts, 8, 128),
            vmem(parts, rows, 128),
            vmem(parts, rows, 128),
            vmem(parts, streams, rows, 128),
            vmem(parts, streams, rows, 128),
            pltpu.VMEM((8, 128), jnp.int32),
            pltpu.SMEM((8, 128), jnp.int32),
            dma((parts,)),
            dma((parts,)),
            dma((parts,)),
            dma((parts, 4)),
            dma((parts, 4)),
            dma((parts, 2, streams)),
            dma((parts, 2, streams)),
            dma((parts,)),
            dma((5,)),
        ],
        compiler_params=pltpu.CompilerParams(
            collective_id=1, has_side_effects=True, vmem_limit_bytes=56 * 1024 * 1024
        ),
        name="overset_step",
    )(flow, speed, char_scale, span_ratio, *small)
    result = result.reshape(width, parts, rows_y // 8, tiles_z, 8, 128)
    result = jnp.swapaxes(result, 3, 4).reshape(width, parts, rows_y, width_z)
    return jnp.transpose(result, (0, 2, 1, 3))[None]


def solution(mesh):
    return jax.shard_map(
        on_device,
        mesh=mesh,
        in_specs=(
            P("block", "stream", None, None, "span"),
            P("block", "stream", None, "span"),
            P(),
            P(),
            P("block", "span", "stream", None, None),
            P("block", "span", "stream", None, None),
            P("block", "span", "stream", None, None),
            P("block", "span", "stream", None, None),
        ),
        out_specs=P("block", "stream", None, None, "span"),
        check_vma=False,
    )
```

```python
import functools

import jax
import jax.numpy as jnp
from jax import lax
from jax.experimental import pallas as pl
from jax.experimental.pallas import tpu as pltpu
from jax.sharding import PartitionSpec as P

MESH = pl.DeviceIdType.MESH
STRIDE = 11
UNROLL = 8
TURN = 4


def limited(first_diff, second_diff):
    low = jnp.minimum(second_diff, 0.0)
    high = jnp.maximum(second_diff, 0.0)
    return jnp.minimum(jnp.maximum(first_diff, low), high)


def kernel(
    sizes,
    flow,
    speed,
    scale,
    ratio,
    send_tile,
    recv_tile,
    recv_live,
    weight,
    field,
    filled,
    donors,
    tiles,
    ws,
    inverse,
    growth,
    blend,
    sending,
    arriving,
    packed,
    row_low,
    row_high,
    col_low,
    col_high,
    last_update,
    last_growth,
    update_in,
    growth_in,
    slot_vmem,
    slot_of,
    load_sem,
    send_sem,
    recv_sem,
    halo_send,
    halo_recv,
    relay_send,
    relay_recv,
    misc_sem,
):
    blocks, spans, streams = sizes
    width, parts, rows, lanes = flow.shape[0], flow.shape[1], flow.shape[2], 128
    peers = blocks * spans
    capacity = send_tile.shape[0]
    tiles_z = rows // 16
    chips = spans // 2
    message = capacity * tiles_z
    b = lax.axis_index("block")
    s = lax.axis_index("span")
    t = lax.axis_index("stream")
    me = b * spans + s
    z, core = s // 2, s % 2
    sign = 1 - 2 * core

    def partner(k):
        offset = (k * STRIDE) % peers
        to_block = (b + sign * (offset // spans) + blocks) % blocks
        to_chip = (z + sign * ((offset % spans) // 2) + chips) % chips
        to_core = (core + offset % 2) % 2
        return to_block, to_chip * 2 + to_core

    def at_stream(target):
        return (b, s, target)

    def load(v):
        return pltpu.make_async_copy(flow.at[:, v], field.at[v], load_sem.at[v])

    first_load = pltpu.make_async_copy(flow.at[:, 0], filled.at[pl.ds(0, width)], misc_sem.at[0])
    first_load.start()
    speed_load = pltpu.make_async_copy(speed, ws.at[pl.ds(1, width)], misc_sem.at[1])
    speed_load.start()
    for v in range(parts):
        load(v).start()

    barrier = pltpu.get_barrier_semaphore()

    def greet(k, carry):
        to_block, to_span = partner(k)
        pl.semaphore_signal(
            barrier, inc=1, device_id=(to_block, to_span, t), device_id_type=MESH
        )
        return carry

    lax.fori_loop(1, peers, greet, 0)
    for j in range(1, streams):
        pl.semaphore_signal(
            barrier, inc=1, device_id=at_stream((t + j) % streams), device_id_type=MESH
        )

    def donor_copy(v, k):
        to_block, to_span = partner(k)
        return pltpu.make_async_remote_copy(
            src_ref=sending.at[v, k],
            dst_ref=arriving.at[v, me],
            send_sem=send_sem.at[v],
            recv_sem=recv_sem.at[v],
            device_id=(to_block, to_span, t),
            device_id_type=MESH,
        )

    def send_all(v, source):
        def lay(x, carry):
            for y in range(16):
                row = pl.ds((y // 8) * 8 * tiles_z + y % 8, tiles_z, stride=8)
                tiles[x * 16 + y] = filled[x, row, :] if source is filled else source[v, x, row, :]
            return carry

        lax.fori_loop(0, width, lay, 0)
        if source is filled:
            pl.semaphore_wait(barrier, peers - 1 + streams - 1)
        for c in range(capacity):
            arriving[v, me, pl.ds(c * tiles_z, tiles_z), :] = tiles[send_tile[c, me]]

        def one(k, carry):
            to_block, to_span = partner(k)
            peer = to_block * spans + to_span
            for c in range(capacity):
                sending[v, k, pl.ds(c * tiles_z, tiles_z), :] = tiles[send_tile[c, peer]]
            donor_copy(v, k).start()
            return carry

        lax.fori_loop(1, peers, one, 0)

    first_load.wait()
    send_all(0, filled)

    speed_load.wait()
    speed_halo = pltpu.make_async_remote_copy(
        src_ref=ws.at[width],
        dst_ref=ws.at[0],
        send_sem=misc_sem.at[2],
        recv_sem=misc_sem.at[3],
        device_id=at_stream((t + 1) % streams),
        device_id_type=MESH,
    )

    @pl.when(t < streams - 1)
    def _():
        speed_halo.start()

    for v in range(parts):
        load(v).wait()
    send_all(1, field)

    @pl.when(t == 0)
    def _():
        ws[0] = jnp.zeros((rows, lanes), jnp.float32)
        row_low[...] = jnp.zeros(row_low.shape, jnp.float32)

    @pl.when(t == streams - 1)
    def _():
        row_high[...] = jnp.zeros(row_high.shape, jnp.float32)

    @pl.when(s == 0)
    def _():
        col_low[...] = jnp.zeros(col_low.shape, jnp.float32)

    @pl.when(s == spans - 1)
    def _():
        col_high[...] = jnp.zeros(col_high.shape, jnp.float32)

    lane = lax.broadcasted_iota(jnp.int32, (8, lanes), 1)
    tile_id = lane * 8 + lax.broadcasted_iota(jnp.int32, (8, lanes), 0)

    def place(g, carry):
        slots, weights = carry
        for c in range(capacity):
            target = jnp.where(recv_live[c, g] == 1, recv_tile[c, g], -1)
            hit = tile_id == target
            slots = jnp.where(hit, g * capacity + c, slots)
            weights = jnp.where(hit, weight[c, g], weights)
        return slots, weights

    slots, weights = lax.fori_loop(
        0,
        peers,
        place,
        (jnp.zeros((8, lanes), jnp.int32), jnp.zeros((8, lanes), jnp.float32)),
    )
    slot_vmem[...] = slots
    to_scalar = pltpu.make_async_copy(slot_vmem, slot_of, misc_sem.at[4])
    to_scalar.start()

    def spread(outer, weights):
        for k in range(2 * TURN):
            i = outer * 2 * TURN + k
            turned = pltpu.roll(weights, (lanes - i) % lanes, 1)
            blend[outer * TURN + k // 2, pl.ds(k % 2 * 8, 8), :] = jnp.broadcast_to(
                turned[:, 0:1], (8, lanes)
            )
        return weights

    lax.fori_loop(0, width // TURN, spread, weights)
    to_scalar.wait()

    @pl.when(t > 0)
    def _():
        speed_halo.wait_recv()

    tile_rows = [pl.ds(i * 8, 8) for i in range(rows // 8)]

    def factors(v):
        rate = scale[v]
        slot = v % 2

        def one(x, carry):
            new = []
            for i, r in enumerate(tile_rows):
                prior = rate * ws[x, r, :]
                here = rate * ws[x + 1, r, :]
                inv = 100.0 / (1.0 + 100.0 * here)
                inverse[x, r, :] = inv
                grown = carry[i] * (prior * inv)
                growth[slot, x, r, :] = grown
                new.append(grown)
            return tuple(new)

        ones = tuple(jnp.ones((8, lanes), jnp.float32) for _ in tile_rows)
        ended = lax.fori_loop(0, width, one, ones)
        for r, grown in zip(tile_rows, ended):
            last_growth[v, r, :] = grown

    def relay(v, kind, j):
        source = last_growth if kind else last_update
        target = growth_in if kind else update_in
        return pltpu.make_async_remote_copy(
            src_ref=source.at[v],
            dst_ref=target.at[v, t],
            send_sem=relay_send.at[v, kind, j],
            recv_sem=relay_recv.at[v, kind, t],
            device_id=at_stream((t + j) % streams),
            device_id_type=MESH,
        )

    def relay_from(v, kind, source):
        target = growth_in if kind else update_in
        return pltpu.make_async_copy(
            target.at[v, source], target.at[v, source], relay_recv.at[v, kind, source]
        )

    def relay_all(v, kind):
        for j in range(1, streams):

            @pl.when(t + j < streams)
            def _():
                relay(v, kind, j).start()

    def fill(v):
        def take_peer(g, carry):
            for c in range(capacity):
                donors[g * capacity + c] = arriving[v, g, pl.ds(c * tiles_z, tiles_z), :]
            return carry

        lax.fori_loop(0, peers, take_peer, 0)

        def scatter(x, carry):
            for y in range(16):
                row = pl.ds((y // 8) * 8 * tiles_z + y % 8, tiles_z, stride=8)
                filled[x, row, :] = donors[slot_of[y % 8, x * 2 + y // 8]]
            return carry

        lax.fori_loop(0, width, scatter, 0)

        def mix(outer, carry):
            first, before, last = carry
            for k in range(2 * TURN):
                x, half = outer * TURN + k // 2, k % 2
                w = blend[x, pl.ds(half * 8, 8), :]
                rest = 1.0 - w
                kept = []
                for i in range(tiles_z):
                    r = tile_rows[half * tiles_z + i]
                    value = rest * field[v, x, r, :] + w * filled[x, r, :]
                    filled[x, r, :] = value
                    kept.append(value)
                i = outer * 2 * TURN + k
                here = lane == i
                first = jnp.where(here, pltpu.roll(kept[0], i, 1), first)
                before = jnp.where(here, pltpu.roll(kept[-1], (i + 2) % lanes, 1), before)
                last = jnp.where(here, pltpu.roll(kept[-1], (i + 1) % lanes, 1), last)
            return first, before, last

        zero = jnp.zeros((8, lanes), jnp.float32)
        for i, value in enumerate(lax.fori_loop(0, width // TURN, mix, (zero, zero, zero))):
            packed[v, i] = value

    def halo_copy(v, kind):
        src, dst, target = (
            (filled.at[pl.ds(width - 2, 2)], row_low.at[v], (b, s, (t + 1) % streams)),
            (filled.at[0], row_high.at[v], (b, s, (t + streams - 1) % streams)),
            (packed.at[v, pl.ds(1, 2)], col_low.at[v], (b, (s + 1) % spans, t)),
            (packed.at[v, 0], col_high.at[v], (b, (s + spans - 1) % spans, t)),
        )[kind]
        return pltpu.make_async_remote_copy(
            src_ref=src,
            dst_ref=dst,
            send_sem=halo_send.at[v, kind],
            recv_sem=halo_recv.at[v, kind],
            device_id=target,
            device_id_type=MESH,
        )

    sends = (t < streams - 1, t > 0, s < spans - 1, s > 0)
    receives = (t > 0, t < streams - 1, s > 0, s < spans - 1)

    def halos(v, which, act):
        for kind in range(4):

            @pl.when(which[kind])
            def _():
                act(halo_copy(v, kind))

    def sweep(v):
        rate = scale[v]
        rate_z = rate * ratio[v]
        is_first = lane == 0
        is_last = lane == lanes - 1
        before2, before1, after1 = col_low[v, 0], col_low[v, 1], col_high[v]
        edge_face = before1 + 0.5 * limited(before1 - before2, packed[v, 0] - before1)
        for i, r in enumerate(tile_rows):
            filled[width, r, :] = row_high[v, r, :]

        for half in range(2):
            mine = tile_rows[half * tiles_z : (half + 1) * tiles_z]

            def step(x, carry, end):
                cells, diffs, flux = carry
                n = range(tiles_z)
                i = x * 2 + half
                to_first = (lanes - i) % lanes
                outside = pltpu.roll(before1, to_first, 1)
                outside_face = pltpu.roll(edge_face, to_first, 1)
                beyond = pltpu.roll(after1, lanes - 1 - i, 1)
                right = [pltpu.roll(u, 1, 1) for u in cells]
                left = [pltpu.roll(u, lanes - 1, 1) for u in cells]
                low = [jnp.where(is_first, ([outside] + right)[i], right[i]) for i in n]
                high = [jnp.where(is_last, (left + [beyond])[i + 1], left[i]) for i in n]
                face = [
                    cells[i] + 0.5 * limited(cells[i] - low[i], high[i] - cells[i]) for i in n
                ]
                shifted = [pltpu.roll(f, 1, 1) for f in face]
                behind = [
                    jnp.where(is_first, ([outside_face] + shifted)[i], shifted[i]) for i in n
                ]
                span_term = [rate_z * (behind[i] - face[i]) for i in n]
                coming = [filled[x + 1, r, :] for r in mine]
                next_diffs = [coming[i] - cells[i] for i in n]
                face_x = [cells[i] + 0.5 * limited(diffs[i], next_diffs[i]) for i in n]
                speed_x = [rate * ws[x + 1, r, :] for r in mine]
                rest = [span_term[i] - speed_x[i] * face_x[i] for i in n]
                update = [inverse[x, r, :] * (flux[i] + rest[i]) for i, r in enumerate(mine)]
                next_flux = [speed_x[i] * (update[i] + face_x[i]) for i in n]
                for i, r in enumerate(mine):
                    field[v, x, r, :] = cells[i] + update[i]
                    if end:
                        last_update[v, r, :] = update[i]
                return coming, next_diffs, next_flux

            def steps(outer, carry):
                for k in range(UNROLL):
                    carry = step(outer * UNROLL + k, carry, k == UNROLL - 1)
                return carry

            cells = [filled[0, r, :] for r in mine]
            up1 = [row_low[v, 1, r, :] for r in mine]
            up2 = [row_low[v, 0, r, :] for r in mine]
            diffs = [c - u for c, u in zip(cells, up1)]
            flux = [
                rate * ws[0, r, :] * (u + 0.5 * limited(u - u2, d))
                for r, u, u2, d in zip(mine, up1, up2, diffs)
            ]

            lax.fori_loop(0, width // UNROLL, steps, (cells, diffs, flux))

    def finish(v):
        slot = v % 2
        for j in range(streams - 1):

            @pl.when(j < t)
            def _():
                relay_from(v, 0, j).wait()
                relay_from(v, 1, j).wait()

        inflow = [jnp.zeros((8, lanes), jnp.float32) for _ in tile_rows]
        for j in range(streams - 1):
            inflow = [
                jnp.where(
                    j < t, growth_in[v, j, r, :] * inflow[i] + update_in[v, j, r, :], inflow[i]
                )
                for i, r in enumerate(tile_rows)
            ]

        def one(x, carry):
            for i, r in enumerate(tile_rows):
                field[v, x, r, :] = field[v, x, r, :] + growth[slot, x, r, :] * inflow[i]
            return carry

        lax.fori_loop(0, width, one, 0)

    def all_donors(v):
        return pltpu.make_async_remote_copy(
            src_ref=sending.at[v, pl.ds(1, peers - 1)],
            dst_ref=arriving.at[v, pl.ds(0, peers - 1)],
            send_sem=send_sem.at[v],
            recv_sem=recv_sem.at[v],
            device_id=(b, s, (t + 1) % streams),
            device_id_type=MESH,
        )

    def variable(v, carry):
        factors(v)
        relay_all(v, 1)
        all_donors(v).wait_recv()
        fill(v)
        halos(v, sends, lambda copy: copy.start())

        @pl.when(v + 2 < parts)
        def _():
            send_all(v + 2, field)

        @pl.when(v > 0)
        def _():
            finish(v - 1)

        halos(v, receives, lambda copy: copy.wait_recv())
        sweep(v)
        relay_all(v, 0)
        halos(v, sends, lambda copy: copy.wait_send())
        return carry

    lax.fori_loop(0, parts, variable, 0)
    finish(parts - 1)

    for v in range(parts):
        all_donors(v).wait_send()
        for kind in range(2):
            for j in range(1, streams):

                @pl.when(t + j < streams)
                def _():
                    relay(v, kind, j).wait_send()

    @pl.when(t < streams - 1)
    def _():
        speed_halo.wait_send()


def write_out(result, out, sems):
    copies = [
        pltpu.make_async_copy(result.at[v], out.at[:, v], sems.at[v])
        for v in range(result.shape[0])
    ]
    for copy in copies:
        copy.start()
    for copy in copies:
        copy.wait()


def on_device(
    flow_state, wave_speed, char_scale, span_ratio, send_tile, recv_tile, recv_live, interp_weight
):
    sizes = tuple(lax.axis_size(a) for a in ("block", "span", "stream"))
    blocks, spans, streams = sizes
    _, width, rows_y, parts, width_z = flow_state.shape
    tiles_z = width_z // 128
    rows = rows_y * tiles_z
    capacity = send_tile.shape[-1]
    peers = blocks * spans

    def tiled(array):
        lead = array.shape[:-2]
        array = array.reshape(lead + (rows_y // 8, 8, tiles_z, 128))
        return jnp.swapaxes(array, -3, -2).reshape(lead + (rows, 128))

    flow = tiled(jnp.transpose(flow_state[0], (0, 2, 1, 3)))
    speed = tiled(wave_speed[0])
    small = [
        jnp.transpose(a.reshape(peers, capacity))
        for a in (send_tile, recv_tile, recv_live, interp_weight)
    ]
    f32 = jnp.float32
    anywhere = pl.BlockSpec(memory_space=pl.ANY)
    scalars = pl.BlockSpec(memory_space=pltpu.SMEM)
    message = capacity * tiles_z
    vmem = lambda *shape: pltpu.VMEM(shape, f32)
    dma = pltpu.SemaphoreType.DMA
    result = pl.pallas_call(
        functools.partial(kernel, sizes),
        out_shape=pltpu.VMEM((parts, width, rows, 128), f32),
        in_specs=[anywhere, anywhere] + [scalars] * 6,
        out_specs=pl.BlockSpec(memory_space=pltpu.VMEM),
        scratch_shapes=[
            vmem(width + 1, rows, 128),
            vmem(peers * capacity, tiles_z, 128),
            vmem(width * rows_y, tiles_z, 128),
            vmem(width + 1, rows, 128),
            vmem(width, rows, 128),
            vmem(2, width, rows, 128),
            vmem(width, rows_y, 128),
            vmem(parts, peers, message, 128),
            vmem(parts, peers, message, 128),
            vmem(parts, 3, 8, 128),
            vmem(parts, 2, rows, 128),
            vmem(parts, rows, 128),
            vmem(parts, 2, 8, 128),
            vmem(parts, 8, 128),
            vmem(parts, rows, 128),
            vmem(parts, rows, 128),
            vmem(parts, streams, rows, 128),
            vmem(parts, streams, rows, 128),
            pltpu.VMEM((8, 128), jnp.int32),
            pltpu.SMEM((8, 128), jnp.int32),
            dma((parts,)),
            dma((parts,)),
            dma((parts,)),
            dma((parts, 4)),
            dma((parts, 4)),
            dma((parts, 2, streams)),
            dma((parts, 2, streams)),
            dma((5,)),
        ],
        compiler_params=pltpu.CompilerParams(
            collective_id=1, has_side_effects=True, vmem_limit_bytes=44 * 1024 * 1024
        ),
        name="overset_step",
    )(flow, speed, char_scale, span_ratio, *small)
    result = pl.pallas_call(
        write_out,
        out_shape=jax.ShapeDtypeStruct(flow.shape, f32),
        in_specs=[pl.BlockSpec(memory_space=pltpu.VMEM)],
        out_specs=pl.BlockSpec(memory_space=pltpu.HBM),
        scratch_shapes=[dma((parts,))],
        compiler_params=pltpu.CompilerParams(vmem_limit_bytes=8 * 1024 * 1024),
        name="write_out",
    )(pltpu.with_memory_space_constraint(result, pltpu.VMEM))
    result = result.reshape(width, parts, rows_y // 8, tiles_z, 8, 128)
    result = jnp.swapaxes(result, 3, 4).reshape(width, parts, rows_y, width_z)
    return jnp.transpose(result, (0, 2, 1, 3))[None]


def solution(mesh):
    return jax.shard_map(
        on_device,
        mesh=mesh,
        in_specs=(
            P("block", "stream", None, None, "span"),
            P("block", "stream", None, "span"),
            P(),
            P(),
            P("block", "span", "stream", None, None),
            P("block", "span", "stream", None, None),
            P("block", "span", "stream", None, None),
            P("block", "span", "stream", None, None),
        ),
        out_specs=P("block", "stream", None, None, "span"),
        check_vma=False,
    )
```

```python
import functools

import jax
import jax.numpy as jnp
from jax import lax
from jax.experimental import pallas as pl
from jax.experimental.pallas import tpu as pltpu
from jax.sharding import PartitionSpec as P

MESH = pl.DeviceIdType.MESH
STRIDE = 11
UNROLL = 8
TURN = 8


def limited(first_diff, second_diff):
    low = jnp.minimum(second_diff, 0.0)
    high = jnp.maximum(second_diff, 0.0)
    return jnp.minimum(jnp.maximum(first_diff, low), high)


def kernel(
    sizes,
    flow,
    speed,
    scale,
    ratio,
    send_tile,
    recv_tile,
    recv_live,
    weight,
    field,
    filled,
    donors,
    tiles,
    laid,
    ws,
    inverse,
    growth,
    blend,
    sending,
    arriving,
    packed,
    row_low,
    row_high,
    col_low,
    col_high,
    last_update,
    last_growth,
    update_in,
    growth_in,
    slot_vmem,
    slot_of,
    load_sem,
    send_sem,
    recv_sem,
    halo_send,
    halo_recv,
    relay_send,
    relay_recv,
    misc_sem,
):
    blocks, spans, streams = sizes
    width, parts, rows, lanes = flow.shape[0], flow.shape[1], flow.shape[2], 128
    peers = blocks * spans
    capacity = send_tile.shape[0]
    tiles_z = rows // 16
    chips = spans // 2
    message = capacity * tiles_z
    b = lax.axis_index("block")
    s = lax.axis_index("span")
    t = lax.axis_index("stream")
    me = b * spans + s
    z, core = s // 2, s % 2
    sign = 1 - 2 * core

    def partner(k):
        offset = (k * STRIDE) % peers
        to_block = (b + sign * (offset // spans) + blocks) % blocks
        to_chip = (z + sign * ((offset % spans) // 2) + chips) % chips
        to_core = (core + offset % 2) % 2
        return to_block, to_chip * 2 + to_core

    def at_stream(target):
        return (b, s, target)

    def load(v):
        return pltpu.make_async_copy(flow.at[:, v], field.at[v], load_sem.at[v])

    first_load = pltpu.make_async_copy(flow.at[:, 0], filled.at[0, pl.ds(0, width)], misc_sem.at[0])
    first_load.start()
    speed_load = pltpu.make_async_copy(speed, ws.at[pl.ds(1, width)], misc_sem.at[1])
    speed_load.start()
    for v in range(parts):
        load(v).start()

    barrier = pltpu.get_barrier_semaphore()

    def greet(k, carry):
        to_block, to_span = partner(k)
        pl.semaphore_signal(
            barrier, inc=1, device_id=(to_block, to_span, t), device_id_type=MESH
        )
        return carry

    lax.fori_loop(1, peers, greet, 0)
    for j in range(1, streams):
        pl.semaphore_signal(
            barrier, inc=1, device_id=at_stream((t + j) % streams), device_id_type=MESH
        )

    def donor_copy(v, k):
        to_block, to_span = partner(k)
        return pltpu.make_async_remote_copy(
            src_ref=sending.at[v, k],
            dst_ref=arriving.at[v, me],
            send_sem=send_sem.at[v],
            recv_sem=recv_sem.at[v],
            device_id=(to_block, to_span, t),
            device_id_type=MESH,
        )

    def send_all(v, source):
        def lay(outer, carry):
            for k in range(16 * TURN):
                x, y = outer * TURN + k // 16, k % 16
                row = pl.ds((y // 8) * 8 * tiles_z + y % 8, tiles_z, stride=8)
                tiles[x * 16 + y] = filled[0, x, row, :] if source is filled else source[v, x, row, :]
            return carry

        lax.fori_loop(0, width // TURN, lay, 0)
        if source is filled:
            pl.semaphore_wait(barrier, peers - 1 + streams - 1)
        for c in range(capacity):
            arriving[v, me, pl.ds(c * tiles_z, tiles_z), :] = tiles[send_tile[c, me]]

        def one(k, carry):
            to_block, to_span = partner(k)
            peer = to_block * spans + to_span
            for c in range(capacity):
                sending[v, k, pl.ds(c * tiles_z, tiles_z), :] = tiles[send_tile[c, peer]]
            donor_copy(v, k).start()
            return carry

        lax.fori_loop(1, peers, one, 0)

    first_load.wait()
    send_all(0, filled)

    speed_load.wait()
    speed_halo = pltpu.make_async_remote_copy(
        src_ref=ws.at[width],
        dst_ref=ws.at[0],
        send_sem=misc_sem.at[2],
        recv_sem=misc_sem.at[3],
        device_id=at_stream((t + 1) % streams),
        device_id_type=MESH,
    )

    @pl.when(t < streams - 1)
    def _():
        speed_halo.start()

    for v in range(parts):
        load(v).wait()
    send_all(1, field)

    @pl.when(t == 0)
    def _():
        ws[0] = jnp.zeros((rows, lanes), jnp.float32)
        row_low[...] = jnp.zeros(row_low.shape, jnp.float32)

    @pl.when(t == streams - 1)
    def _():
        row_high[...] = jnp.zeros(row_high.shape, jnp.float32)

    @pl.when(s == 0)
    def _():
        col_low[...] = jnp.zeros(col_low.shape, jnp.float32)

    @pl.when(s == spans - 1)
    def _():
        col_high[...] = jnp.zeros(col_high.shape, jnp.float32)

    lane = lax.broadcasted_iota(jnp.int32, (8, lanes), 1)
    tile_id = lane * 8 + lax.broadcasted_iota(jnp.int32, (8, lanes), 0)

    def place(g, carry):
        slots, weights = carry
        for c in range(capacity):
            target = jnp.where(recv_live[c, g] == 1, recv_tile[c, g], -1)
            hit = tile_id == target
            slots = jnp.where(hit, g * capacity + c, slots)
            weights = jnp.where(hit, weight[c, g], weights)
        return slots, weights

    slots, weights = lax.fori_loop(
        0,
        peers,
        place,
        (jnp.zeros((8, lanes), jnp.int32), jnp.zeros((8, lanes), jnp.float32)),
    )
    slot_vmem[...] = slots
    to_scalar = pltpu.make_async_copy(slot_vmem, slot_of, misc_sem.at[4])
    to_scalar.start()

    def spread(outer, weights):
        for k in range(2 * TURN):
            i = outer * 2 * TURN + k
            turned = pltpu.roll(weights, (lanes - i) % lanes, 1)
            blend[outer * TURN + k // 2, pl.ds(k % 2 * 8, 8), :] = jnp.broadcast_to(
                turned[:, 0:1], (8, lanes)
            )
        return weights

    lax.fori_loop(0, width // TURN, spread, weights)
    to_scalar.wait()

    @pl.when(t > 0)
    def _():
        speed_halo.wait_recv()

    tile_rows = [pl.ds(i * 8, 8) for i in range(rows // 8)]

    def factors(v):
        rate = scale[v]
        half, slot = v % 2, v % 3

        def one(x, carry):
            new = []
            for i, r in enumerate(tile_rows):
                prior = rate * ws[x, r, :]
                here = rate * ws[x + 1, r, :]
                inv = 100.0 / (1.0 + 100.0 * here)
                inverse[half, x, r, :] = inv
                grown = carry[i] * (prior * inv)
                growth[slot, x, r, :] = grown
                new.append(grown)
            return tuple(new)

        def several(outer, carry):
            for k in range(TURN):
                carry = one(outer * TURN + k, carry)
            return carry

        ones = tuple(jnp.ones((8, lanes), jnp.float32) for _ in tile_rows)
        ended = lax.fori_loop(0, width // TURN, several, ones)
        for r, grown in zip(tile_rows, ended):
            last_growth[v, r, :] = grown

    def relay(v, kind, j):
        source = last_growth if kind else last_update
        target = growth_in if kind else update_in
        return pltpu.make_async_remote_copy(
            src_ref=source.at[v],
            dst_ref=target.at[v, t],
            send_sem=relay_send.at[v, kind, j],
            recv_sem=relay_recv.at[v, kind, t],
            device_id=at_stream((t + j) % streams),
            device_id_type=MESH,
        )

    def relay_from(v, kind, source):
        target = growth_in if kind else update_in
        return pltpu.make_async_copy(
            target.at[v, source], target.at[v, source], relay_recv.at[v, kind, source]
        )

    def relay_all(v, kind):
        for j in range(1, streams):

            @pl.when(t + j < streams)
            def _():
                relay(v, kind, j).start()

    def fill(v):
        turn = v % 2

        def take_peer(g, carry):
            for c in range(capacity):
                donors[g * capacity + c] = arriving[v, g, pl.ds(c * tiles_z, tiles_z), :]
            return carry

        lax.fori_loop(0, peers, take_peer, 0)

        def scatter(outer):
            for k in range(16 * TURN):
                x, y = outer * TURN + k // 16, k % 16
                row = pl.ds((y // 8) * 8 * tiles_z + y % 8, tiles_z, stride=8)
                laid[x, row, :] = donors[slot_of[y % 8, x * 2 + y // 8]]

        def mix(outer, carry):
            first, before, last = carry
            for k in range(2 * TURN):
                x, half = outer * TURN + k // 2, k % 2
                w = blend[x, pl.ds(half * 8, 8), :]
                rest = 1.0 - w
                kept = []
                for i in range(tiles_z):
                    r = tile_rows[half * tiles_z + i]
                    value = rest * field[v, x, r, :] + w * laid[x, r, :]
                    filled[turn, x, r, :] = value
                    kept.append(value)
                i = outer * 2 * TURN + k
                here = lane == i
                first = jnp.where(here, pltpu.roll(kept[0], i, 1), first)
                before = jnp.where(here, pltpu.roll(kept[-1], (i + 2) % lanes, 1), before)
                last = jnp.where(here, pltpu.roll(kept[-1], (i + 1) % lanes, 1), last)
            return first, before, last

        def both(outer, carry):
            carry = mix(outer, carry)
            scatter(outer + 1)
            return carry

        zero = jnp.zeros((8, lanes), jnp.float32)
        scatter(0)
        edges = lax.fori_loop(0, width // TURN - 1, both, (zero, zero, zero))
        for i, value in enumerate(mix(width // TURN - 1, edges)):
            packed[v, i] = value

    def halo_copy(v, kind):
        src, dst, target = (
            (filled.at[v % 2, pl.ds(width - 2, 2)], row_low.at[v], (b, s, (t + 1) % streams)),
            (filled.at[v % 2, 0], row_high.at[v], (b, s, (t + streams - 1) % streams)),
            (packed.at[v, pl.ds(1, 2)], col_low.at[v], (b, (s + 1) % spans, t)),
            (packed.at[v, 0], col_high.at[v], (b, (s + spans - 1) % spans, t)),
        )[kind]
        return pltpu.make_async_remote_copy(
            src_ref=src,
            dst_ref=dst,
            send_sem=halo_send.at[v, kind],
            recv_sem=halo_recv.at[v, kind],
            device_id=target,
            device_id_type=MESH,
        )

    sends = (t < streams - 1, t > 0, s < spans - 1, s > 0)
    receives = (t > 0, t < streams - 1, s > 0, s < spans - 1)

    def halos(v, which, act):
        for kind in range(4):

            @pl.when(which[kind])
            def _():
                act(halo_copy(v, kind))

    def sweep(v):
        turn = v % 2
        rate = scale[v]
        rate_z = rate * ratio[v]
        is_first = lane == 0
        is_last = lane == lanes - 1
        before2, before1, after1 = col_low[v, 0], col_low[v, 1], col_high[v]
        edge_face = before1 + 0.5 * limited(before1 - before2, packed[v, 0] - before1)
        for i, r in enumerate(tile_rows):
            filled[turn, width, r, :] = row_high[v, r, :]

        for half in range(2):
            mine = tile_rows[half * tiles_z : (half + 1) * tiles_z]

            def step(x, carry, end):
                cells, diffs, flux = carry
                n = range(tiles_z)
                i = x * 2 + half
                to_first = (lanes - i) % lanes
                outside = pltpu.roll(before1, to_first, 1)
                outside_face = pltpu.roll(edge_face, to_first, 1)
                beyond = pltpu.roll(after1, lanes - 1 - i, 1)
                right = [pltpu.roll(u, 1, 1) for u in cells]
                left = [pltpu.roll(u, lanes - 1, 1) for u in cells]
                low = [jnp.where(is_first, ([outside] + right)[i], right[i]) for i in n]
                high = [jnp.where(is_last, (left + [beyond])[i + 1], left[i]) for i in n]
                face = [
                    cells[i] + 0.5 * limited(cells[i] - low[i], high[i] - cells[i]) for i in n
                ]
                shifted = [pltpu.roll(f, 1, 1) for f in face]
                behind = [
                    jnp.where(is_first, ([outside_face] + shifted)[i], shifted[i]) for i in n
                ]
                span_term = [rate_z * (behind[i] - face[i]) for i in n]
                coming = [filled[turn, x + 1, r, :] for r in mine]
                next_diffs = [coming[i] - cells[i] for i in n]
                face_x = [cells[i] + 0.5 * limited(diffs[i], next_diffs[i]) for i in n]
                speed_x = [rate * ws[x + 1, r, :] for r in mine]
                rest = [span_term[i] - speed_x[i] * face_x[i] for i in n]
                update = [inverse[turn, x, r, :] * (flux[i] + rest[i]) for i, r in enumerate(mine)]
                next_flux = [speed_x[i] * (update[i] + face_x[i]) for i in n]
                for i, r in enumerate(mine):
                    field[v, x, r, :] = cells[i] + update[i]
                    if end:
                        last_update[v, r, :] = update[i]
                return coming, next_diffs, next_flux

            def steps(outer, carry):
                for k in range(UNROLL):
                    carry = step(outer * UNROLL + k, carry, k == UNROLL - 1)
                return carry

            cells = [filled[turn, 0, r, :] for r in mine]
            up1 = [row_low[v, 1, r, :] for r in mine]
            up2 = [row_low[v, 0, r, :] for r in mine]
            diffs = [c - u for c, u in zip(cells, up1)]
            flux = [
                rate * ws[0, r, :] * (u + 0.5 * limited(u - u2, d))
                for r, u, u2, d in zip(mine, up1, up2, diffs)
            ]

            lax.fori_loop(0, width // UNROLL, steps, (cells, diffs, flux))

    def finish(v):
        slot = v % 3
        for j in range(streams - 1):

            @pl.when(j < t)
            def _():
                relay_from(v, 0, j).wait()
                relay_from(v, 1, j).wait()

        inflow = [jnp.zeros((8, lanes), jnp.float32) for _ in tile_rows]
        for j in range(streams - 1):
            inflow = [
                jnp.where(
                    j < t, growth_in[v, j, r, :] * inflow[i] + update_in[v, j, r, :], inflow[i]
                )
                for i, r in enumerate(tile_rows)
            ]

        def one(outer, carry):
            for k in range(TURN):
                x = outer * TURN + k
                new = [
                    field[v, x, r, :] + growth[slot, x, r, :] * inflow[i]
                    for i, r in enumerate(tile_rows)
                ]
                for r, value in zip(tile_rows, new):
                    field[v, x, r, :] = value
            return carry

        lax.fori_loop(0, width // TURN, one, 0)

    def all_donors(v):
        return pltpu.make_async_remote_copy(
            src_ref=sending.at[v, pl.ds(1, peers - 1)],
            dst_ref=arriving.at[v, pl.ds(0, peers - 1)],
            send_sem=send_sem.at[v],
            recv_sem=recv_sem.at[v],
            device_id=(b, s, (t + 1) % streams),
            device_id_type=MESH,
        )

    def march(v):
        halos(v, receives, lambda copy: copy.wait_recv())
        sweep(v)
        relay_all(v, 0)
        halos(v, sends, lambda copy: copy.wait_send())

    def variable(v, carry):
        all_donors(v).wait_recv()
        fill(v)
        halos(v, sends, lambda copy: copy.start())

        @pl.when(v + 2 < parts)
        def _():
            send_all(v + 2, field)

        @pl.when(v > 0)
        def _():
            march(v - 1)

        @pl.when(v + 1 < parts)
        def _():
            factors(v + 1)
            relay_all(v + 1, 1)

            @pl.when(v > 0)
            def _():
                finish(v - 1)

        return carry

    factors(0)
    relay_all(0, 1)
    lax.fori_loop(0, parts, variable, 0)
    march(parts - 1)
    finish(parts - 2)
    finish(parts - 1)

    for v in range(parts):
        all_donors(v).wait_send()
        for kind in range(2):
            for j in range(1, streams):

                @pl.when(t + j < streams)
                def _():
                    relay(v, kind, j).wait_send()

    @pl.when(t < streams - 1)
    def _():
        speed_halo.wait_send()


def write_out(result, out, sems):
    copies = [
        pltpu.make_async_copy(result.at[v], out.at[:, v], sems.at[v])
        for v in range(result.shape[0])
    ]
    for copy in copies:
        copy.start()
    for copy in copies:
        copy.wait()


def on_device(
    flow_state, wave_speed, char_scale, span_ratio, send_tile, recv_tile, recv_live, interp_weight
):
    sizes = tuple(lax.axis_size(a) for a in ("block", "span", "stream"))
    blocks, spans, streams = sizes
    _, width, rows_y, parts, width_z = flow_state.shape
    tiles_z = width_z // 128
    rows = rows_y * tiles_z
    capacity = send_tile.shape[-1]
    peers = blocks * spans

    def tiled(array):
        lead = array.shape[:-2]
        array = array.reshape(lead + (rows_y // 8, 8, tiles_z, 128))
        return jnp.swapaxes(array, -3, -2).reshape(lead + (rows, 128))

    flow = tiled(jnp.transpose(flow_state[0], (0, 2, 1, 3)))
    speed = tiled(wave_speed[0])
    small = [
        jnp.transpose(a.reshape(peers, capacity))
        for a in (send_tile, recv_tile, recv_live, interp_weight)
    ]
    f32 = jnp.float32
    anywhere = pl.BlockSpec(memory_space=pl.ANY)
    scalars = pl.BlockSpec(memory_space=pltpu.SMEM)
    message = capacity * tiles_z
    vmem = lambda *shape: pltpu.VMEM(shape, f32)
    dma = pltpu.SemaphoreType.DMA
    result = pl.pallas_call(
        functools.partial(kernel, sizes),
        out_shape=pltpu.VMEM((parts, width, rows, 128), f32),
        in_specs=[anywhere, anywhere] + [scalars] * 6,
        out_specs=pl.BlockSpec(memory_space=pltpu.VMEM),
        scratch_shapes=[
            vmem(2, width + 1, rows, 128),
            vmem(peers * capacity, tiles_z, 128),
            vmem(width * rows_y, tiles_z, 128),
            vmem(width, rows, 128),
            vmem(width + 1, rows, 128),
            vmem(2, width, rows, 128),
            vmem(3, width, rows, 128),
            vmem(width, rows_y, 128),
            vmem(parts, peers, message, 128),
            vmem(parts, peers, message, 128),
            vmem(parts, 3, 8, 128),
            vmem(parts, 2, rows, 128),
            vmem(parts, rows, 128),
            vmem(parts, 2, 8, 128),
            vmem(parts, 8, 128),
            vmem(parts, rows, 128),
            vmem(parts, rows, 128),
            vmem(parts, streams, rows, 128),
            vmem(parts, streams, rows, 128),
            pltpu.VMEM((8, 128), jnp.int32),
            pltpu.SMEM((8, 128), jnp.int32),
            dma((parts,)),
            dma((parts,)),
            dma((parts,)),
            dma((parts, 4)),
            dma((parts, 4)),
            dma((parts, 2, streams)),
            dma((parts, 2, streams)),
            dma((5,)),
        ],
        compiler_params=pltpu.CompilerParams(
            collective_id=1, has_side_effects=True, vmem_limit_bytes=48 * 1024 * 1024
        ),
        name="overset_step",
    )(flow, speed, char_scale, span_ratio, *small)
    result = pl.pallas_call(
        write_out,
        out_shape=jax.ShapeDtypeStruct(flow.shape, f32),
        in_specs=[pl.BlockSpec(memory_space=pltpu.VMEM)],
        out_specs=pl.BlockSpec(memory_space=pltpu.HBM),
        scratch_shapes=[dma((parts,))],
        compiler_params=pltpu.CompilerParams(vmem_limit_bytes=8 * 1024 * 1024),
        name="write_out",
    )(pltpu.with_memory_space_constraint(result, pltpu.VMEM))
    result = result.reshape(width, parts, rows_y // 8, tiles_z, 8, 128)
    result = jnp.swapaxes(result, 3, 4).reshape(width, parts, rows_y, width_z)
    return jnp.transpose(result, (0, 2, 1, 3))[None]


def solution(mesh):
    return jax.shard_map(
        on_device,
        mesh=mesh,
        in_specs=(
            P("block", "stream", None, None, "span"),
            P("block", "stream", None, "span"),
            P(),
            P(),
            P("block", "span", "stream", None, None),
            P("block", "span", "stream", None, None),
            P("block", "span", "stream", None, None),
            P("block", "span", "stream", None, None),
        ),
        out_specs=P("block", "stream", None, None, "span"),
        check_vma=False,
    )
```

```python
import functools

import jax
import jax.numpy as jnp
from jax import lax
from jax.experimental import pallas as pl
from jax.experimental.pallas import tpu as pltpu
from jax.sharding import PartitionSpec as P

MESH = pl.DeviceIdType.MESH
STRIDE = 11
UNROLL = 8
TURN = 8


def limited(first_diff, second_diff):
    low = jnp.minimum(second_diff, 0.0)
    high = jnp.maximum(second_diff, 0.0)
    return jnp.minimum(jnp.maximum(first_diff, low), high)


def kernel(
    sizes,
    flow,
    speed,
    scale,
    ratio,
    send_tile,
    recv_tile,
    recv_live,
    weight,
    field,
    filled,
    donors,
    tiles,
    laid,
    ws,
    inverse,
    growth,
    blend,
    sending,
    arriving,
    packed,
    row_low,
    row_high,
    col_low,
    col_high,
    last_update,
    last_growth,
    update_in,
    growth_in,
    slot_vmem,
    slot_of,
    load_sem,
    send_sem,
    recv_sem,
    halo_send,
    halo_recv,
    relay_send,
    relay_recv,
    misc_sem,
):
    blocks, spans, streams = sizes
    width, parts, rows, lanes = flow.shape[0], flow.shape[1], flow.shape[2], 128
    peers = blocks * spans
    capacity = send_tile.shape[0]
    tiles_z = rows // 16
    chips = spans // 2
    message = capacity * tiles_z
    b = lax.axis_index("block")
    s = lax.axis_index("span")
    t = lax.axis_index("stream")
    me = b * spans + s
    z, core = s // 2, s % 2
    sign = 1 - 2 * core

    def partner(k):
        offset = (k * STRIDE) % peers
        to_block = (b + sign * (offset // spans) + blocks) % blocks
        to_chip = (z + sign * ((offset % spans) // 2) + chips) % chips
        to_core = (core + offset % 2) % 2
        return to_block, to_chip * 2 + to_core

    def at_stream(target):
        return (b, s, target)

    def load(v):
        return pltpu.make_async_copy(flow.at[:, v], field.at[v], load_sem.at[v])

    first_load = pltpu.make_async_copy(flow.at[:, 0], filled.at[0, pl.ds(0, width)], misc_sem.at[0])
    first_load.start()
    speed_load = pltpu.make_async_copy(speed, ws.at[pl.ds(1, width)], misc_sem.at[1])

    barrier = pltpu.get_barrier_semaphore()

    def greet(k, carry):
        to_block, to_span = partner(k)
        pl.semaphore_signal(
            barrier, inc=1, device_id=(to_block, to_span, t), device_id_type=MESH
        )
        return carry

    lax.fori_loop(1, peers, greet, 0)
    for j in range(1, streams):
        pl.semaphore_signal(
            barrier, inc=1, device_id=at_stream((t + j) % streams), device_id_type=MESH
        )

    def donor_copy(v, k):
        to_block, to_span = partner(k)
        return pltpu.make_async_remote_copy(
            src_ref=sending.at[v, k],
            dst_ref=arriving.at[v, me],
            send_sem=send_sem.at[v],
            recv_sem=recv_sem.at[v],
            device_id=(to_block, to_span, t),
            device_id_type=MESH,
        )

    def send_all(v, source):
        def lay(outer, carry):
            for k in range(16 * TURN):
                x, y = outer * TURN + k // 16, k % 16
                row = pl.ds((y // 8) * 8 * tiles_z + y % 8, tiles_z, stride=8)
                tiles[x * 16 + y] = filled[0, x, row, :] if source is filled else source[v, x, row, :]
            return carry

        lax.fori_loop(0, width // TURN, lay, 0)
        if source is filled:
            pl.semaphore_wait(barrier, peers - 1 + streams - 1)
        for c in range(capacity):
            arriving[v, me, pl.ds(c * tiles_z, tiles_z), :] = tiles[send_tile[c, me]]

        def one(k, carry):
            to_block, to_span = partner(k)
            peer = to_block * spans + to_span
            for c in range(capacity):
                sending[v, k, pl.ds(c * tiles_z, tiles_z), :] = tiles[send_tile[c, peer]]
            donor_copy(v, k).start()
            return carry

        lax.fori_loop(1, peers, one, 0)

    first_load.wait()
    speed_load.start()
    for v in range(parts):
        load(v).start()
    send_all(0, filled)

    speed_load.wait()
    speed_halo = pltpu.make_async_remote_copy(
        src_ref=ws.at[width],
        dst_ref=ws.at[0],
        send_sem=misc_sem.at[2],
        recv_sem=misc_sem.at[3],
        device_id=at_stream((t + 1) % streams),
        device_id_type=MESH,
    )

    @pl.when(t < streams - 1)
    def _():
        speed_halo.start()

    for v in range(parts):
        load(v).wait()
    send_all(1, field)

    @pl.when(t == 0)
    def _():
        ws[0] = jnp.zeros((rows, lanes), jnp.float32)
        row_low[...] = jnp.zeros(row_low.shape, jnp.float32)

    @pl.when(t == streams - 1)
    def _():
        row_high[...] = jnp.zeros(row_high.shape, jnp.float32)

    @pl.when(s == 0)
    def _():
        col_low[...] = jnp.zeros(col_low.shape, jnp.float32)

    @pl.when(s == spans - 1)
    def _():
        col_high[...] = jnp.zeros(col_high.shape, jnp.float32)

    lane = lax.broadcasted_iota(jnp.int32, (8, lanes), 1)
    tile_id = lane * 8 + lax.broadcasted_iota(jnp.int32, (8, lanes), 0)

    def place(g, carry):
        slots, weights = carry
        for c in range(capacity):
            target = jnp.where(recv_live[c, g] == 1, recv_tile[c, g], -1)
            hit = tile_id == target
            slots = jnp.where(hit, g * capacity + c, slots)
            weights = jnp.where(hit, weight[c, g], weights)
        return slots, weights

    slots, weights = lax.fori_loop(
        0,
        peers,
        place,
        (jnp.zeros((8, lanes), jnp.int32), jnp.zeros((8, lanes), jnp.float32)),
    )
    slot_vmem[...] = slots
    to_scalar = pltpu.make_async_copy(slot_vmem, slot_of, misc_sem.at[4])
    to_scalar.start()

    def spread(outer, weights):
        for k in range(2 * TURN):
            i = outer * 2 * TURN + k
            turned = pltpu.roll(weights, (lanes - i) % lanes, 1)
            blend[outer * TURN + k // 2, pl.ds(k % 2 * 8, 8), :] = jnp.broadcast_to(
                turned[:, 0:1], (8, lanes)
            )
        return weights

    lax.fori_loop(0, width // TURN, spread, weights)
    to_scalar.wait()

    @pl.when(t > 0)
    def _():
        speed_halo.wait_recv()

    tile_rows = [pl.ds(i * 8, 8) for i in range(rows // 8)]
    half_rows = [pl.ds(i * (rows // 2), rows // 2) for i in range(2)]

    def factors(v):
        rate = scale[v]
        half, slot = v % 2, v % 3

        def one(x, carry):
            new = []
            for i, r in enumerate(tile_rows):
                prior = rate * ws[x, r, :]
                here = rate * ws[x + 1, r, :]
                inv = 100.0 / (1.0 + 100.0 * here)
                inverse[half, x, r, :] = inv
                grown = carry[i] * (prior * inv)
                growth[slot, x, r, :] = grown
                new.append(grown)
            return tuple(new)

        def several(outer, carry):
            for k in range(TURN):
                carry = one(outer * TURN + k, carry)
            return carry

        ones = tuple(jnp.ones((8, lanes), jnp.float32) for _ in tile_rows)
        ended = lax.fori_loop(0, width // TURN, several, ones)
        for r, grown in zip(tile_rows, ended):
            last_growth[v, r, :] = grown

    def relay(v, kind, j):
        source = last_growth if kind == 2 else last_update
        target = growth_in if kind == 2 else update_in
        part = pl.ds(0, rows) if kind == 2 else half_rows[kind]
        return pltpu.make_async_remote_copy(
            src_ref=source.at[v, part],
            dst_ref=target.at[v, t, part],
            send_sem=relay_send.at[v, kind, j],
            recv_sem=relay_recv.at[v, kind, t],
            device_id=at_stream((t + j) % streams),
            device_id_type=MESH,
        )

    def relay_from(v, kind, source):
        target = growth_in if kind == 2 else update_in
        part = pl.ds(0, rows) if kind == 2 else half_rows[kind]
        return pltpu.make_async_copy(
            target.at[v, source, part], target.at[v, source, part], relay_recv.at[v, kind, source]
        )

    def relay_all(v, kind):
        for j in range(1, streams):

            @pl.when(t + j < streams)
            def _():
                relay(v, kind, j).start()

    def fill(v, half):
        turn = v % 2
        group = 2 * TURN
        mine = tile_rows[half * tiles_z : (half + 1) * tiles_z]

        def take_peer(g, carry):
            for c in range(capacity):
                donors[g * capacity + c] = arriving[v, g, pl.ds(c * tiles_z, tiles_z), :]
            return carry

        if half == 0:
            lax.fori_loop(0, peers, take_peer, 0)

        def scatter(outer):
            for k in range(8 * group):
                x, y = outer * group + k // 8, k % 8
                row = pl.ds(half * (rows // 2) + y, tiles_z, stride=8)
                laid[x, row, :] = donors[slot_of[y, x * 2 + half]]

        def mix(outer, carry):
            first, before, last = carry
            for k in range(group):
                x = outer * group + k
                w = blend[x, pl.ds(half * 8, 8), :]
                rest = 1.0 - w
                kept = []
                for r in mine:
                    value = rest * field[v, x, r, :] + w * laid[x, r, :]
                    filled[turn, x, r, :] = value
                    kept.append(value)
                here = lane == x
                first = jnp.where(here, pltpu.roll(kept[0], x, 1), first)
                before = jnp.where(here, pltpu.roll(kept[-1], (x + 2) % lanes, 1), before)
                last = jnp.where(here, pltpu.roll(kept[-1], (x + 1) % lanes, 1), last)
            return first, before, last

        def both(outer, carry):
            carry = mix(outer, carry)
            scatter(outer + 1)
            return carry

        zero = jnp.zeros((8, lanes), jnp.float32)
        scatter(0)
        edges = lax.fori_loop(0, width // group - 1, both, (zero, zero, zero))
        for i, value in enumerate(mix(width // group - 1, edges)):
            packed[v, half, i] = value

    def halo_copy(v, half, kind):
        part = half_rows[half]
        src, dst, target = (
            (
                filled.at[v % 2, pl.ds(width - 2, 2), part],
                row_low.at[v, pl.ds(0, 2), part],
                (b, s, (t + 1) % streams),
            ),
            (
                filled.at[v % 2, 0, part],
                row_high.at[v, part],
                (b, s, (t + streams - 1) % streams),
            ),
            (packed.at[v, half, pl.ds(1, 2)], col_low.at[v, half], (b, (s + 1) % spans, t)),
            (packed.at[v, half, 0], col_high.at[v, half], (b, (s + spans - 1) % spans, t)),
        )[kind]
        return pltpu.make_async_remote_copy(
            src_ref=src,
            dst_ref=dst,
            send_sem=halo_send.at[v, half, kind],
            recv_sem=halo_recv.at[v, half, kind],
            device_id=target,
            device_id_type=MESH,
        )

    sends = (t < streams - 1, t > 0, s < spans - 1, s > 0)
    receives = (t > 0, t < streams - 1, s > 0, s < spans - 1)

    def halos(v, half, which, act):
        for kind in range(4):

            @pl.when(which[kind])
            def _():
                act(halo_copy(v, half, kind))

    def sweep(v, half):
        turn = v % 2
        rate = scale[v]
        rate_z = rate * ratio[v]
        is_first = lane == 0
        is_last = lane == lanes - 1
        before2, before1, after1 = col_low[v, half, 0], col_low[v, half, 1], col_high[v, half]
        edge_face = before1 + 0.5 * limited(before1 - before2, packed[v, half, 0] - before1)
        mine = tile_rows[half * tiles_z : (half + 1) * tiles_z]
        for r in mine:
            filled[turn, width, r, :] = row_high[v, r, :]

        def step(x, carry, end):
            cells, diffs, flux = carry
            n = range(tiles_z)
            to_first = (lanes - x) % lanes
            outside = pltpu.roll(before1, to_first, 1)
            outside_face = pltpu.roll(edge_face, to_first, 1)
            beyond = pltpu.roll(after1, lanes - 1 - x, 1)
            right = [pltpu.roll(u, 1, 1) for u in cells]
            left = [pltpu.roll(u, lanes - 1, 1) for u in cells]
            low = [jnp.where(is_first, ([outside] + right)[i], right[i]) for i in n]
            high = [jnp.where(is_last, (left + [beyond])[i + 1], left[i]) for i in n]
            face = [
                cells[i] + 0.5 * limited(cells[i] - low[i], high[i] - cells[i]) for i in n
            ]
            shifted = [pltpu.roll(f, 1, 1) for f in face]
            behind = [
                jnp.where(is_first, ([outside_face] + shifted)[i], shifted[i]) for i in n
            ]
            span_term = [rate_z * (behind[i] - face[i]) for i in n]
            coming = [filled[turn, x + 1, r, :] for r in mine]
            next_diffs = [coming[i] - cells[i] for i in n]
            face_x = [cells[i] + 0.5 * limited(diffs[i], next_diffs[i]) for i in n]
            speed_x = [rate * ws[x + 1, r, :] for r in mine]
            rest = [span_term[i] - speed_x[i] * face_x[i] for i in n]
            update = [inverse[turn, x, r, :] * (flux[i] + rest[i]) for i, r in enumerate(mine)]
            next_flux = [speed_x[i] * (update[i] + face_x[i]) for i in n]
            for i, r in enumerate(mine):
                field[v, x, r, :] = cells[i] + update[i]
                if end:
                    last_update[v, r, :] = update[i]
            return coming, next_diffs, next_flux

        def steps(outer, carry):
            for k in range(UNROLL):
                carry = step(outer * UNROLL + k, carry, k == UNROLL - 1)
            return carry

        cells = [filled[turn, 0, r, :] for r in mine]
        up1 = [row_low[v, 1, r, :] for r in mine]
        up2 = [row_low[v, 0, r, :] for r in mine]
        diffs = [c - u for c, u in zip(cells, up1)]
        flux = [
            rate * ws[0, r, :] * (u + 0.5 * limited(u - u2, d))
            for r, u, u2, d in zip(mine, up1, up2, diffs)
        ]

        lax.fori_loop(0, width // UNROLL, steps, (cells, diffs, flux))

    def finish(v, half):
        slot = v % 3
        mine = tile_rows[half * tiles_z : (half + 1) * tiles_z]
        for j in range(streams - 1):

            @pl.when(j < t)
            def _():
                relay_from(v, half, j).wait()
                if half == 0:
                    relay_from(v, 2, j).wait()

        inflow = [jnp.zeros((8, lanes), jnp.float32) for _ in mine]
        for j in range(streams - 1):
            inflow = [
                jnp.where(
                    j < t, growth_in[v, j, r, :] * inflow[i] + update_in[v, j, r, :], inflow[i]
                )
                for i, r in enumerate(mine)
            ]

        def one(outer, carry):
            for k in range(TURN):
                x = outer * TURN + k
                new = [
                    field[v, x, r, :] + growth[slot, x, r, :] * inflow[i]
                    for i, r in enumerate(mine)
                ]
                for r, value in zip(mine, new):
                    field[v, x, r, :] = value
            return carry

        lax.fori_loop(0, width // TURN, one, 0)

    def all_donors(v):
        return pltpu.make_async_remote_copy(
            src_ref=sending.at[v, pl.ds(1, peers - 1)],
            dst_ref=arriving.at[v, pl.ds(0, peers - 1)],
            send_sem=send_sem.at[v],
            recv_sem=recv_sem.at[v],
            device_id=(b, s, (t + 1) % streams),
            device_id_type=MESH,
        )

    def variable(v, carry):
        all_donors(v).wait_recv()
        for half in range(2):
            fill(v, half)
            halos(v, half, sends, lambda copy: copy.start())

        @pl.when(v + 2 < parts)
        def _():
            send_all(v + 2, field)

        @pl.when(v + 1 < parts)
        def _():
            factors(v + 1)
            relay_all(v + 1, 2)

        @pl.when(v > 0)
        def _():
            finish(v - 1, 0)
            finish(v - 1, 1)

        for half in range(2):
            halos(v, half, receives, lambda copy: copy.wait_recv())
            sweep(v, half)
            relay_all(v, half)
        for half in range(2):
            halos(v, half, sends, lambda copy: copy.wait_send())
        return carry

    factors(0)
    relay_all(0, 2)
    lax.fori_loop(0, parts, variable, 0)
    for half in range(2):
        finish(parts - 1, half)

    for v in range(parts):
        all_donors(v).wait_send()
        for kind in range(3):
            for j in range(1, streams):

                @pl.when(t + j < streams)
                def _():
                    relay(v, kind, j).wait_send()

    @pl.when(t < streams - 1)
    def _():
        speed_halo.wait_send()


def write_out(result, out, sems):
    copies = [
        pltpu.make_async_copy(result.at[v], out.at[:, v], sems.at[v])
        for v in range(result.shape[0])
    ]
    for copy in copies:
        copy.start()
    for copy in copies:
        copy.wait()


def on_device(
    flow_state, wave_speed, char_scale, span_ratio, send_tile, recv_tile, recv_live, interp_weight
):
    sizes = tuple(lax.axis_size(a) for a in ("block", "span", "stream"))
    blocks, spans, streams = sizes
    _, width, rows_y, parts, width_z = flow_state.shape
    tiles_z = width_z // 128
    rows = rows_y * tiles_z
    capacity = send_tile.shape[-1]
    peers = blocks * spans

    def tiled(array):
        lead = array.shape[:-2]
        array = array.reshape(lead + (rows_y // 8, 8, tiles_z, 128))
        return jnp.swapaxes(array, -3, -2).reshape(lead + (rows, 128))

    flow = tiled(jnp.transpose(flow_state[0], (0, 2, 1, 3)))
    speed = tiled(wave_speed[0])
    small = [
        jnp.transpose(a.reshape(peers, capacity))
        for a in (send_tile, recv_tile, recv_live, interp_weight)
    ]
    f32 = jnp.float32
    anywhere = pl.BlockSpec(memory_space=pl.ANY)
    scalars = pl.BlockSpec(memory_space=pltpu.SMEM)
    message = capacity * tiles_z
    vmem = lambda *shape: pltpu.VMEM(shape, f32)
    dma = pltpu.SemaphoreType.DMA
    result = pl.pallas_call(
        functools.partial(kernel, sizes),
        out_shape=pltpu.VMEM((parts, width, rows, 128), f32),
        in_specs=[anywhere, anywhere] + [scalars] * 6,
        out_specs=pl.BlockSpec(memory_space=pltpu.VMEM),
        scratch_shapes=[
            vmem(2, width + 1, rows, 128),
            vmem(peers * capacity, tiles_z, 128),
            vmem(width * rows_y, tiles_z, 128),
            vmem(width, rows, 128),
            vmem(width + 1, rows, 128),
            vmem(2, width, rows, 128),
            vmem(3, width, rows, 128),
            vmem(width, rows_y, 128),
            vmem(parts, peers, message, 128),
            vmem(parts, peers, message, 128),
            vmem(parts, 2, 3, 8, 128),
            vmem(parts, 2, rows, 128),
            vmem(parts, rows, 128),
            vmem(parts, 2, 2, 8, 128),
            vmem(parts, 2, 8, 128),
            vmem(parts, rows, 128),
            vmem(parts, rows, 128),
            vmem(parts, streams, rows, 128),
            vmem(parts, streams, rows, 128),
            pltpu.VMEM((8, 128), jnp.int32),
            pltpu.SMEM((8, 128), jnp.int32),
            dma((parts,)),
            dma((parts,)),
            dma((parts,)),
            dma((parts, 2, 4)),
            dma((parts, 2, 4)),
            dma((parts, 3, streams)),
            dma((parts, 3, streams)),
            dma((5,)),
        ],
        compiler_params=pltpu.CompilerParams(
            collective_id=1, has_side_effects=True, vmem_limit_bytes=48 * 1024 * 1024
        ),
        name="overset_step",
    )(flow, speed, char_scale, span_ratio, *small)
    result = pl.pallas_call(
        write_out,
        out_shape=jax.ShapeDtypeStruct(flow.shape, f32),
        in_specs=[pl.BlockSpec(memory_space=pltpu.VMEM)],
        out_specs=pl.BlockSpec(memory_space=pltpu.HBM),
        scratch_shapes=[dma((parts,))],
        compiler_params=pltpu.CompilerParams(vmem_limit_bytes=8 * 1024 * 1024),
        name="write_out",
    )(pltpu.with_memory_space_constraint(result, pltpu.VMEM))
    result = result.reshape(width, parts, rows_y // 8, tiles_z, 8, 128)
    result = jnp.swapaxes(result, 3, 4).reshape(width, parts, rows_y, width_z)
    return jnp.transpose(result, (0, 2, 1, 3))[None]


def solution(mesh):
    return jax.shard_map(
        on_device,
        mesh=mesh,
        in_specs=(
            P("block", "stream", None, None, "span"),
            P("block", "stream", None, "span"),
            P(),
            P(),
            P("block", "span", "stream", None, None),
            P("block", "span", "stream", None, None),
            P("block", "span", "stream", None, None),
            P("block", "span", "stream", None, None),
        ),
        out_specs=P("block", "stream", None, None, "span"),
        check_vma=False,
    )
```

```python
import functools

import jax
import jax.numpy as jnp
from jax import lax
from jax.experimental import pallas as pl
from jax.experimental.pallas import tpu as pltpu
from jax.sharding import PartitionSpec as P

MESH = pl.DeviceIdType.MESH
STRIDE = 11
UNROLL = 8
TURN = 8


def limited(first_diff, second_diff):
    low = jnp.minimum(second_diff, 0.0)
    high = jnp.maximum(second_diff, 0.0)
    return jnp.minimum(jnp.maximum(first_diff, low), high)


def kernel(
    sizes,
    flow,
    speed,
    scale,
    ratio,
    send_tile,
    recv_tile,
    recv_live,
    weight,
    field,
    filled,
    donors,
    tiles,
    laid,
    ws,
    inverse,
    growth,
    blend,
    sending,
    arriving,
    packed,
    row_low,
    row_high,
    col_low,
    col_high,
    last_update,
    last_growth,
    update_in,
    growth_in,
    slot_vmem,
    slot_of,
    load_sem,
    send_sem,
    recv_sem,
    halo_send,
    halo_recv,
    relay_send,
    relay_recv,
    misc_sem,
):
    blocks, spans, streams = sizes
    width, parts, rows, lanes = flow.shape[0], flow.shape[1], flow.shape[2], 128
    peers = blocks * spans
    capacity = send_tile.shape[0]
    tiles_z = rows // 16
    chips = spans // 2
    message = capacity * tiles_z
    b = lax.axis_index("block")
    s = lax.axis_index("span")
    t = lax.axis_index("stream")
    me = b * spans + s
    z, core = s // 2, s % 2
    sign = 1 - 2 * core

    def partner(k):
        offset = (k * STRIDE) % peers
        to_block = (b + sign * (offset // spans) + blocks) % blocks
        to_chip = (z + sign * ((offset % spans) // 2) + chips) % chips
        to_core = (core + offset % 2) % 2
        return to_block, to_chip * 2 + to_core

    def at_stream(target):
        return (b, s, target)

    def load(v):
        return pltpu.make_async_copy(flow.at[:, v], field.at[v], load_sem.at[v])

    first_load = pltpu.make_async_copy(flow.at[:, 0], filled.at[0, pl.ds(0, width)], misc_sem.at[0])
    first_load.start()
    speed_load = pltpu.make_async_copy(speed, ws.at[pl.ds(1, width)], misc_sem.at[1])

    barrier = pltpu.get_barrier_semaphore()

    def greet(k, carry):
        to_block, to_span = partner(k)
        pl.semaphore_signal(
            barrier, inc=1, device_id=(to_block, to_span, t), device_id_type=MESH
        )
        return carry

    lax.fori_loop(1, peers, greet, 0)
    for j in range(1, streams):
        pl.semaphore_signal(
            barrier, inc=1, device_id=at_stream((t + j) % streams), device_id_type=MESH
        )

    def donor_copy(v, k):
        to_block, to_span = partner(k)
        return pltpu.make_async_remote_copy(
            src_ref=sending.at[v, k],
            dst_ref=arriving.at[v, me],
            send_sem=send_sem.at[v],
            recv_sem=recv_sem.at[v],
            device_id=(to_block, to_span, t),
            device_id_type=MESH,
        )

    def send_all(v, source):
        def lay(outer, carry):
            for k in range(16 * TURN):
                x, y = outer * TURN + k // 16, k % 16
                row = pl.ds((y // 8) * 8 * tiles_z + y % 8, tiles_z, stride=8)
                tiles[x * 16 + y] = filled[0, x, row, :] if source is filled else source[v, x, row, :]
            return carry

        lax.fori_loop(0, width // TURN, lay, 0)
        if source is filled:
            pl.semaphore_wait(barrier, peers - 1 + streams - 1)
        for c in range(capacity):
            arriving[v, me, pl.ds(c * tiles_z, tiles_z), :] = tiles[send_tile[c, me]]

        def one(k, carry):
            to_block, to_span = partner(k)
            peer = to_block * spans + to_span
            for c in range(capacity):
                sending[v, k, pl.ds(c * tiles_z, tiles_z), :] = tiles[send_tile[c, peer]]
            donor_copy(v, k).start()
            return carry

        lax.fori_loop(1, peers, one, 0)

    first_load.wait()
    speed_load.start()
    for v in range(parts):
        load(v).start()
    send_all(0, filled)

    speed_load.wait()
    speed_halo = pltpu.make_async_remote_copy(
        src_ref=ws.at[width],
        dst_ref=ws.at[0],
        send_sem=misc_sem.at[2],
        recv_sem=misc_sem.at[3],
        device_id=at_stream((t + 1) % streams),
        device_id_type=MESH,
    )

    @pl.when(t < streams - 1)
    def _():
        speed_halo.start()

    for v in range(parts):
        load(v).wait()
    send_all(1, field)

    @pl.when(t == 0)
    def _():
        ws[0] = jnp.zeros((rows, lanes), jnp.float32)
        row_low[...] = jnp.zeros(row_low.shape, jnp.float32)

    @pl.when(t == streams - 1)
    def _():
        row_high[...] = jnp.zeros(row_high.shape, jnp.float32)

    @pl.when(s == 0)
    def _():
        col_low[...] = jnp.zeros(col_low.shape, jnp.float32)

    @pl.when(s == spans - 1)
    def _():
        col_high[...] = jnp.zeros(col_high.shape, jnp.float32)

    lane = lax.broadcasted_iota(jnp.int32, (8, lanes), 1)
    tile_id = lane * 8 + lax.broadcasted_iota(jnp.int32, (8, lanes), 0)

    def place(g, carry):
        slots, weights = carry
        for c in range(capacity):
            target = jnp.where(recv_live[c, g] == 1, recv_tile[c, g], -1)
            hit = tile_id == target
            slots = jnp.where(hit, g * capacity + c, slots)
            weights = jnp.where(hit, weight[c, g], weights)
        return slots, weights

    slots, weights = lax.fori_loop(
        0,
        peers,
        place,
        (jnp.zeros((8, lanes), jnp.int32), jnp.zeros((8, lanes), jnp.float32)),
    )
    slot_vmem[...] = slots
    to_scalar = pltpu.make_async_copy(slot_vmem, slot_of, misc_sem.at[4])
    to_scalar.start()

    def spread(outer, weights):
        for k in range(2 * TURN):
            i = outer * 2 * TURN + k
            turned = pltpu.roll(weights, (lanes - i) % lanes, 1)
            blend[outer * TURN + k // 2, pl.ds(k % 2 * 8, 8), :] = jnp.broadcast_to(
                turned[:, 0:1], (8, lanes)
            )
        return weights

    lax.fori_loop(0, width // TURN, spread, weights)
    to_scalar.wait()

    @pl.when(t > 0)
    def _():
        speed_halo.wait_recv()

    tile_rows = [pl.ds(i * 8, 8) for i in range(rows // 8)]

    def factors(v):
        rate = scale[v]
        half, slot = v % 2, v % 3

        def one(x, carry):
            new = []
            for i, r in enumerate(tile_rows):
                prior = rate * ws[x, r, :]
                here = rate * ws[x + 1, r, :]
                inv = 100.0 / (1.0 + 100.0 * here)
                inverse[half, x, r, :] = inv
                grown = carry[i] * (prior * inv)
                growth[slot, x, r, :] = grown
                new.append(grown)
            return tuple(new)

        def several(outer, carry):
            for k in range(TURN):
                carry = one(outer * TURN + k, carry)
            return carry

        ones = tuple(jnp.ones((8, lanes), jnp.float32) for _ in tile_rows)
        ended = lax.fori_loop(0, width // TURN, several, ones)
        for r, grown in zip(tile_rows, ended):
            last_growth[v, r, :] = grown

    def relay(v, kind, j):
        source = last_growth if kind else last_update
        target = growth_in if kind else update_in
        return pltpu.make_async_remote_copy(
            src_ref=source.at[v],
            dst_ref=target.at[v, t],
            send_sem=relay_send.at[v, kind, j],
            recv_sem=relay_recv.at[v, kind, t],
            device_id=at_stream((t + j) % streams),
            device_id_type=MESH,
        )

    def relay_from(v, kind, source):
        target = growth_in if kind else update_in
        return pltpu.make_async_copy(
            target.at[v, source], target.at[v, source], relay_recv.at[v, kind, source]
        )

    def relay_all(v, kind):
        for j in range(1, streams):

            @pl.when(t + j < streams)
            def _():
                relay(v, kind, j).start()

    def fill(v):
        turn = v % 2

        def take_peer(g, carry):
            for c in range(capacity):
                donors[g * capacity + c] = arriving[v, g, pl.ds(c * tiles_z, tiles_z), :]
            return carry

        lax.fori_loop(0, peers, take_peer, 0)

        def scatter(outer):
            for k in range(16 * TURN):
                x, y = outer * TURN + k // 16, k % 16
                row = pl.ds((y // 8) * 8 * tiles_z + y % 8, tiles_z, stride=8)
                laid[x, row, :] = donors[slot_of[y % 8, x * 2 + y // 8]]

        def mix(outer, carry):
            first, before, last = carry
            for k in range(2 * TURN):
                x, half = outer * TURN + k // 2, k % 2
                w = blend[x, pl.ds(half * 8, 8), :]
                rest = 1.0 - w
                kept = []
                for i in range(tiles_z):
                    r = tile_rows[half * tiles_z + i]
                    value = rest * field[v, x, r, :] + w * laid[x, r, :]
                    filled[turn, x, r, :] = value
                    kept.append(value)
                i = outer * 2 * TURN + k
                here = lane == i
                first = jnp.where(here, pltpu.roll(kept[0], i, 1), first)
                before = jnp.where(here, pltpu.roll(kept[-1], (i + 2) % lanes, 1), before)
                last = jnp.where(here, pltpu.roll(kept[-1], (i + 1) % lanes, 1), last)
            return first, before, last

        def both(outer, carry):
            carry = mix(outer, carry)
            scatter(outer + 1)
            return carry

        zero = jnp.zeros((8, lanes), jnp.float32)
        scatter(0)
        edges = lax.fori_loop(0, width // TURN - 1, both, (zero, zero, zero))
        for i, value in enumerate(mix(width // TURN - 1, edges)):
            packed[v, i] = value

    def halo_copy(v, kind):
        src, dst, target = (
            (filled.at[v % 2, pl.ds(width - 2, 2)], row_low.at[v], (b, s, (t + 1) % streams)),
            (filled.at[v % 2, 0], row_high.at[v], (b, s, (t + streams - 1) % streams)),
            (packed.at[v, pl.ds(1, 2)], col_low.at[v], (b, (s + 1) % spans, t)),
            (packed.at[v, 0], col_high.at[v], (b, (s + spans - 1) % spans, t)),
        )[kind]
        return pltpu.make_async_remote_copy(
            src_ref=src,
            dst_ref=dst,
            send_sem=halo_send.at[v, kind],
            recv_sem=halo_recv.at[v, kind],
            device_id=target,
            device_id_type=MESH,
        )

    sends = (t < streams - 1, t > 0, s < spans - 1, s > 0)
    receives = (t > 0, t < streams - 1, s > 0, s < spans - 1)

    def halos(v, which, act):
        for kind in range(4):

            @pl.when(which[kind])
            def _():
                act(halo_copy(v, kind))

    def sweep(v):
        turn = v % 2
        rate = scale[v]
        rate_z = rate * ratio[v]
        is_first = lane == 0
        is_last = lane == lanes - 1
        before2, before1, after1 = col_low[v, 0], col_low[v, 1], col_high[v]
        edge_face = before1 + 0.5 * limited(before1 - before2, packed[v, 0] - before1)
        for i, r in enumerate(tile_rows):
            filled[turn, width, r, :] = row_high[v, r, :]

        for half in range(2):
            mine = tile_rows[half * tiles_z : (half + 1) * tiles_z]

            def step(x, carry, end):
                cells, diffs, flux = carry
                n = range(tiles_z)
                i = x * 2 + half
                to_first = (lanes - i) % lanes
                outside = pltpu.roll(before1, to_first, 1)
                outside_face = pltpu.roll(edge_face, to_first, 1)
                beyond = pltpu.roll(after1, lanes - 1 - i, 1)
                right = [pltpu.roll(u, 1, 1) for u in cells]
                left = [pltpu.roll(u, lanes - 1, 1) for u in cells]
                low = [jnp.where(is_first, ([outside] + right)[i], right[i]) for i in n]
                high = [jnp.where(is_last, (left + [beyond])[i + 1], left[i]) for i in n]
                face = [
                    cells[i] + 0.5 * limited(cells[i] - low[i], high[i] - cells[i]) for i in n
                ]
                shifted = [pltpu.roll(f, 1, 1) for f in face]
                behind = [
                    jnp.where(is_first, ([outside_face] + shifted)[i], shifted[i]) for i in n
                ]
                span_term = [rate_z * (behind[i] - face[i]) for i in n]
                coming = [filled[turn, x + 1, r, :] for r in mine]
                next_diffs = [coming[i] - cells[i] for i in n]
                face_x = [cells[i] + 0.5 * limited(diffs[i], next_diffs[i]) for i in n]
                speed_x = [rate * ws[x + 1, r, :] for r in mine]
                rest = [span_term[i] - speed_x[i] * face_x[i] for i in n]
                update = [inverse[turn, x, r, :] * (flux[i] + rest[i]) for i, r in enumerate(mine)]
                next_flux = [speed_x[i] * (update[i] + face_x[i]) for i in n]
                for i, r in enumerate(mine):
                    field[v, x, r, :] = cells[i] + update[i]
                    if end:
                        last_update[v, r, :] = update[i]
                return coming, next_diffs, next_flux

            def steps(outer, carry):
                for k in range(UNROLL):
                    carry = step(outer * UNROLL + k, carry, k == UNROLL - 1)
                return carry

            cells = [filled[turn, 0, r, :] for r in mine]
            up1 = [row_low[v, 1, r, :] for r in mine]
            up2 = [row_low[v, 0, r, :] for r in mine]
            diffs = [c - u for c, u in zip(cells, up1)]
            flux = [
                rate * ws[0, r, :] * (u + 0.5 * limited(u - u2, d))
                for r, u, u2, d in zip(mine, up1, up2, diffs)
            ]

            lax.fori_loop(0, width // UNROLL, steps, (cells, diffs, flux))

    def finish(v):
        slot = v % 3
        for j in range(streams - 1):

            @pl.when(j < t)
            def _():
                relay_from(v, 0, j).wait()
                relay_from(v, 1, j).wait()

        inflow = [jnp.zeros((8, lanes), jnp.float32) for _ in tile_rows]
        for j in range(streams - 1):
            inflow = [
                jnp.where(
                    j < t, growth_in[v, j, r, :] * inflow[i] + update_in[v, j, r, :], inflow[i]
                )
                for i, r in enumerate(tile_rows)
            ]

        def one(outer, carry):
            for k in range(TURN):
                x = outer * TURN + k
                new = [
                    field[v, x, r, :] + growth[slot, x, r, :] * inflow[i]
                    for i, r in enumerate(tile_rows)
                ]
                for r, value in zip(tile_rows, new):
                    field[v, x, r, :] = value
            return carry

        lax.fori_loop(0, width // TURN, one, 0)

    def all_donors(v):
        return pltpu.make_async_remote_copy(
            src_ref=sending.at[v, pl.ds(1, peers - 1)],
            dst_ref=arriving.at[v, pl.ds(0, peers - 1)],
            send_sem=send_sem.at[v],
            recv_sem=recv_sem.at[v],
            device_id=(b, s, (t + 1) % streams),
            device_id_type=MESH,
        )

    def march(v):
        halos(v, receives, lambda copy: copy.wait_recv())
        sweep(v)
        relay_all(v, 0)
        halos(v, sends, lambda copy: copy.wait_send())

    def variable(v, carry):
        all_donors(v).wait_recv()
        fill(v)
        halos(v, sends, lambda copy: copy.start())

        @pl.when(v > 0)
        def _():
            march(v - 1)

        @pl.when(v + 2 < parts)
        def _():
            send_all(v + 2, field)

        @pl.when(v + 1 < parts)
        def _():
            factors(v + 1)
            relay_all(v + 1, 1)

            @pl.when(v > 0)
            def _():
                finish(v - 1)

        return carry

    factors(0)
    relay_all(0, 1)
    lax.fori_loop(0, parts, variable, 0)
    march(parts - 1)
    finish(parts - 2)
    finish(parts - 1)

    for v in range(parts):
        all_donors(v).wait_send()
        for kind in range(2):
            for j in range(1, streams):

                @pl.when(t + j < streams)
                def _():
                    relay(v, kind, j).wait_send()

    @pl.when(t < streams - 1)
    def _():
        speed_halo.wait_send()


def write_out(result, out, sems):
    copies = [
        pltpu.make_async_copy(result.at[v], out.at[:, v], sems.at[v])
        for v in range(result.shape[0])
    ]
    for copy in copies:
        copy.start()
    for copy in copies:
        copy.wait()


def on_device(
    flow_state, wave_speed, char_scale, span_ratio, send_tile, recv_tile, recv_live, interp_weight
):
    sizes = tuple(lax.axis_size(a) for a in ("block", "span", "stream"))
    blocks, spans, streams = sizes
    _, width, rows_y, parts, width_z = flow_state.shape
    tiles_z = width_z // 128
    rows = rows_y * tiles_z
    capacity = send_tile.shape[-1]
    peers = blocks * spans

    def tiled(array):
        lead = array.shape[:-2]
        array = array.reshape(lead + (rows_y // 8, 8, tiles_z, 128))
        return jnp.swapaxes(array, -3, -2).reshape(lead + (rows, 128))

    flow = tiled(jnp.transpose(flow_state[0], (0, 2, 1, 3)))
    speed = tiled(wave_speed[0])
    small = [
        jnp.transpose(a.reshape(peers, capacity))
        for a in (send_tile, recv_tile, recv_live, interp_weight)
    ]
    f32 = jnp.float32
    anywhere = pl.BlockSpec(memory_space=pl.ANY)
    scalars = pl.BlockSpec(memory_space=pltpu.SMEM)
    message = capacity * tiles_z
    vmem = lambda *shape: pltpu.VMEM(shape, f32)
    dma = pltpu.SemaphoreType.DMA
    result = pl.pallas_call(
        functools.partial(kernel, sizes),
        out_shape=pltpu.VMEM((parts, width, rows, 128), f32),
        in_specs=[anywhere, anywhere] + [scalars] * 6,
        out_specs=pl.BlockSpec(memory_space=pltpu.VMEM),
        scratch_shapes=[
            vmem(2, width + 1, rows, 128),
            vmem(peers * capacity, tiles_z, 128),
            vmem(width * rows_y, tiles_z, 128),
            vmem(width, rows, 128),
            vmem(width + 1, rows, 128),
            vmem(2, width, rows, 128),
            vmem(3, width, rows, 128),
            vmem(width, rows_y, 128),
            vmem(parts, peers, message, 128),
            vmem(parts, peers, message, 128),
            vmem(parts, 3, 8, 128),
            vmem(parts, 2, rows, 128),
            vmem(parts, rows, 128),
            vmem(parts, 2, 8, 128),
            vmem(parts, 8, 128),
            vmem(parts, rows, 128),
            vmem(parts, rows, 128),
            vmem(parts, streams, rows, 128),
            vmem(parts, streams, rows, 128),
            pltpu.VMEM((8, 128), jnp.int32),
            pltpu.SMEM((8, 128), jnp.int32),
            dma((parts,)),
            dma((parts,)),
            dma((parts,)),
            dma((parts, 4)),
            dma((parts, 4)),
            dma((parts, 2, streams)),
            dma((parts, 2, streams)),
            dma((5,)),
        ],
        compiler_params=pltpu.CompilerParams(
            collective_id=1, has_side_effects=True, vmem_limit_bytes=48 * 1024 * 1024
        ),
        name="overset_step",
    )(flow, speed, char_scale, span_ratio, *small)
    result = pl.pallas_call(
        write_out,
        out_shape=jax.ShapeDtypeStruct(flow.shape, f32),
        in_specs=[pl.BlockSpec(memory_space=pltpu.VMEM)],
        out_specs=pl.BlockSpec(memory_space=pltpu.HBM),
        scratch_shapes=[dma((parts,))],
        compiler_params=pltpu.CompilerParams(vmem_limit_bytes=8 * 1024 * 1024),
        name="write_out",
    )(pltpu.with_memory_space_constraint(result, pltpu.VMEM))
    result = result.reshape(width, parts, rows_y // 8, tiles_z, 8, 128)
    result = jnp.swapaxes(result, 3, 4).reshape(width, parts, rows_y, width_z)
    return jnp.transpose(result, (0, 2, 1, 3))[None]


def solution(mesh):
    return jax.shard_map(
        on_device,
        mesh=mesh,
        in_specs=(
            P("block", "stream", None, None, "span"),
            P("block", "stream", None, "span"),
            P(),
            P(),
            P("block", "span", "stream", None, None),
            P("block", "span", "stream", None, None),
            P("block", "span", "stream", None, None),
            P("block", "span", "stream", None, None),
        ),
        out_specs=P("block", "stream", None, None, "span"),
        check_vma=False,
    )
```
